32 devices in a mesh: front: 4 (over x, core), grp: 8 (over z, y).
Axes of the slice: x: 2, y: 2, z: 4, core: 2. Of those that a mesh axis runs over, the one named last changes fastest.
Arguments:
- contributions: bfloat16 [4096, 16384], P(('front', 'grp')), may hold values from -6 to 6
- sketch_matrix: bfloat16 [16384, 256], P(('front', 'grp')), may hold values from -0.046875 to 0.046875
- destinations: int32 [4096, 1], replicated, may hold values from 0 to 31; in each aligned block of 128 rows (0 to 127, 128 to 255, ...) at most 8 rows name the same one
- parent_rows: int32 [4096], replicated, may hold values from 0 to 1023
- front_sizes: int32 [4], P('front'), may hold values from 4096 to 8192
- leaf_skeleton: int32 [4, 8, 128], P('front', 'grp'), may hold values from 0 to 1023, as said below
- merge_skeleton: int32 [4, 7, 128], P('front'), may hold values from 0 to 255, as said below
Outputs:
- leaf_maps: float32 [4, 8192, 128], P('front', 'grp')
- node_maps: float32 [4, 8, 3, 256, 128], P('front', 'grp')
- top_rows: float32 [4, 8, 128, 256], P('front', 'grp')
The draws below stay inside these ranges and needn't reach their ends.
Inputs may be any that keep to these rules, and one draw needn't show every extreme that they name: `destinations`: in the rows of one device no destination is named by more than 8 rows. `leaf_skeleton`: each row holds 128 different row numbers of a leaf block. `merge_skeleton`: each row holds 128 different positions of the stacked 2 * 128 rows.
All inputs are finite; a program needn't handle non-finite values.
Results may differ from the reference program's by a relative error of at most 0.003.
Values may be sent and summed in bfloat16 or wider, within the bound.
A program may use at most 64 MiB of HBM per device.

```python
import math
import jax
import jax.numpy as jnp
import numpy as np
from jax import lax

CHILD_ORDER = 16384
SKETCH = 256
K = 128
PR_DEV = 1024
LEVELS = 3
CHILD_DEV = 128
FRONTS = 4
LEAVES = 8
PROWS = 8192
NODES = 7
CAP = 8
DEVICES = 32


def distinct_rows(key, count, length, keep):
    scores = jax.random.randint(key, (count, length), 0, 2 ** 20) * length + jnp.arange(length, dtype=jnp.int32)[None, :]
    order = jnp.argsort(scores, axis=-1, stable=True)
    return order[:, :keep].astype(jnp.int32)


def draw_leaf_skeleton(key, part):
    picked = distinct_rows(jax.random.fold_in(key, 11), FRONTS * LEAVES, PR_DEV, K)
    return picked.reshape(FRONTS, LEAVES, K)


def draw_merge_skeleton(key, part):
    picked = distinct_rows(jax.random.fold_in(key, 23), FRONTS * NODES, 2 * K, K)
    return picked.reshape(FRONTS, NODES, K)


def place_ends(array, key, low, high):
    dims = array.shape
    index_at = [jax.random.randint(jax.random.fold_in(key, axis), (), 0, dims[axis]) for axis in range(len(dims))]
    array = array.at[tuple(index_at)].set(low)
    longest = dims.index(max(dims))
    index_at[longest] = (index_at[longest] + 1) % dims[longest]
    return array.at[tuple(index_at)].set(high)


def block_levels(rng, extent, split, smallest, largest):
    gain = 1.0
    for axis_at, parts in split:
        steps = jax.random.uniform(jax.random.fold_in(jax.random.fold_in(rng, 6), axis_at), (parts,), jnp.float32, smallest / len(split), largest / len(split))
        gain = gain * jnp.repeat(jnp.exp(steps), extent[axis_at] // parts).reshape((-1,) + (1,) * (len(extent) - 1 - axis_at))
    return gain


def assign_block(rng, own, number, rows, amount, top, bound, skew):
    order = jax.random.permutation(rng, amount)
    heavy_load, common = shares(amount, rows * top, bound, skew, True), shares(amount, rows * top, bound, skew, False)
    places = jnp.arange(amount)

    def named(sizes, offset_by):
        used = int((sizes > 0).sum())
        fixed = max(1, used // 4)
        shifted = fixed + (places - fixed + offset_by * (used - fixed)) % max(1, amount - fixed)
        return jnp.zeros((amount,), jnp.int32).at[order[jnp.where(places < fixed, places, shifted)]].set(jnp.asarray(sizes, jnp.int32))

    sizes = jnp.where(number % 4 == 0, named(heavy_load, number // 4), named(common, number - number // 4 - 1))
    mixed = jax.random.permutation(jax.random.fold_in(own, 3), amount)
    giver, receiver = mixed[0:amount // 2 * 2:2], mixed[1:amount // 2 * 2:2]
    room = jnp.minimum(sizes[giver] - 1, bound - sizes[receiver]) // 2
    room = jnp.where((giver == order[0]) | (receiver == order[0]) | (sizes[receiver] == 0), 0, jnp.maximum(room, 0))
    shifted = jax.random.randint(jax.random.fold_in(own, 4), (amount // 2,), 0, 1 << 20) % (room + 1)
    sizes = sizes.at[giver].add(-shifted).at[receiver].add(shifted)
    labels = jnp.searchsorted(jnp.cumsum(sizes), jnp.arange(rows * top), side="right").astype(jnp.int32)
    table = labels.reshape(top, rows).T
    table = table[jax.random.permutation(jax.random.fold_in(own, 1), rows)]
    offset_by = jax.random.randint(jax.random.fold_in(own, 2), (rows, 1), 0, top)
    return jnp.take_along_axis(table, (jnp.arange(top)[None, :] + offset_by) % top, axis=1)


def shares(count, total, limit, skew, full):
    weights = [(1 << 20) // math.isqrt(standing ** skew) + 1 for standing in range(1, count + 1)]
    largest = limit if full else min(limit, max(-(-total // count), total * weights[0] // sum(weights)))
    least = 1 if total - largest >= count - 1 else 0
    holding, rest = [largest] + [least] * (count - 1), total - largest - least * (count - 1)
    while rest > 0:
        free = [i for i in range(1, count) if holding[i] < largest] or [i for i in range(1, count) if holding[i] < limit]
        whole, left = sum([weights[i] for i in free]), rest
        for i in free:
            more = min(limit - holding[i], max(1, left * weights[i] // whole), rest)
            holding[i] = holding[i] + more
            rest = rest - more
    return np.array(holding)


def noise(stream_key, shape, deviation, reach, pieces=(), kind=jnp.bfloat16):
    array = deviation * jax.random.normal(stream_key, shape, jnp.float32)
    if pieces:
        array = array * block_levels(stream_key, shape, pieces, -0.22, 0.18)
    return jnp.clip(array, -reach, reach).astype(kind)


def setup_inputs(seed: int = 0) -> dict:
    splits = jax.random.split(jax.random.key(seed), 8)
    contributions = noise(splits[0], (DEVICES * CHILD_DEV, CHILD_ORDER), 1.0, 6.0, ((0, 32),))
    sketch_matrix = noise(splits[1], (CHILD_ORDER, SKETCH), CHILD_ORDER ** -0.5, 0.046875, ((0, 32),))
    destinations_keys = jax.random.split(jax.random.fold_in(splits[2], 1), (DEVICES * CHILD_DEV) // CHILD_DEV)
    destinations_turns = jax.random.permutation(jax.random.fold_in(splits[2], 3), (DEVICES * CHILD_DEV) // CHILD_DEV)
    destinations = jax.vmap(lambda own, number: assign_block(jax.random.fold_in(splits[2], 2), own, number, CHILD_DEV, DEVICES, 1, CAP, 1))(destinations_keys, destinations_turns).reshape((DEVICES * CHILD_DEV, 1))
    parent_rows = place_ends(jax.random.randint(splits[3], (DEVICES * CHILD_DEV,), 0, PR_DEV), jax.random.fold_in(splits[3], 1), 0, PR_DEV - 1).astype(jnp.int32)
    front_sizes = place_ends(jax.random.randint(splits[4], (FRONTS,), PROWS // 2, PROWS + 1), jax.random.fold_in(splits[4], 1), PROWS // 2, PROWS).astype(jnp.int32)
    leaf_skeleton = draw_leaf_skeleton(jax.random.fold_in(splits[7], 71), 0)
    merge_skeleton = draw_merge_skeleton(jax.random.fold_in(splits[7], 71), 0)
    return {"contributions": contributions, "sketch_matrix": sketch_matrix, "destinations": destinations, "parent_rows": parent_rows, "front_sizes": front_sizes, "leaf_skeleton": leaf_skeleton, "merge_skeleton": merge_skeleton}


def ridge_map(rows, basis):
    gram = jnp.dot(basis, basis.T, precision=lax.Precision.HIGHEST)
    shift = 0.1 * jnp.mean(jnp.diagonal(gram)) + 1e-5
    ident = jnp.eye(gram.shape[0], dtype=jnp.float32)
    gram = gram + shift * ident
    approx = ident / jnp.trace(gram)
    for step in range(24):
        approx = jnp.dot(approx, 2.0 * ident - jnp.dot(gram, approx, precision=lax.Precision.HIGHEST), precision=lax.Precision.HIGHEST)
    right = jnp.dot(rows, basis.T, precision=lax.Precision.HIGHEST)
    return jnp.dot(right, approx, precision=lax.Precision.HIGHEST)


def reference(contributions, sketch_matrix, destinations, parent_rows, front_sizes, leaf_skeleton, merge_skeleton):
    blocks = contributions.reshape(DEVICES, CHILD_DEV, CHILD_ORDER)
    sketch = lax.map(lambda block: jnp.dot(block, sketch_matrix, preferred_element_type=jnp.float32).astype(jnp.bfloat16), blocks)
    sketch = sketch.reshape(DEVICES * CHILD_DEV, SKETCH).astype(jnp.float32)
    target = destinations[:, 0] * PR_DEV + parent_rows
    parent = jax.ops.segment_sum(sketch, target, num_segments=DEVICES * PR_DEV).reshape(FRONTS, PROWS, SKETCH)
    keep = jnp.arange(PROWS, dtype=jnp.int32)[None, :] < front_sizes[:, None]
    parent = jnp.where(keep[:, :, None], parent, jnp.zeros_like(parent))
    blocks_y = parent.reshape(FRONTS, LEAVES, PR_DEV, SKETCH)
    pick = jax.vmap(jax.vmap(lambda rows, index: jnp.take(rows, index, axis=0)))
    solve = jax.vmap(jax.vmap(ridge_map))
    bases = pick(blocks_y, leaf_skeleton)
    leaf_maps = solve(blocks_y, bases).reshape(FRONTS, PROWS, K)
    count = LEAVES
    level_maps = []
    for level in range(LEVELS):
        offset = LEAVES - count
        stacked = bases.reshape(FRONTS, count // 2, 2 * K, SKETCH)
        chosen = merge_skeleton[:, offset:offset + count // 2]
        bases = pick(stacked, chosen)
        maps = solve(stacked, bases)
        level_maps.append(jnp.repeat(maps, 2 ** (level + 1), axis=1))
        count = count // 2
    node_maps = jnp.stack(level_maps, axis=2)
    top_rows = jnp.repeat(bases, 2 ** LEVELS, axis=1)
    return leaf_maps, node_maps, top_rows
```

```python
import functools
import heapq

import jax
import jax.numpy as jnp
from jax import lax
from jax.experimental import pallas as pl
from jax.experimental.pallas import tpu as pltpu
from jax.sharding import PartitionSpec as P

PR_DEV = 1024
LEVELS = 3
STEPS = 24
EXACT_STEPS = 2
HIGHEST = lax.Precision.HIGHEST
MESH = pl.DeviceIdType.MESH


def bits_of(count):
    return count.bit_length() - 1


def flip(value, mask):
    bit = 1
    while bit <= mask:
        if mask & bit:
            value = value + bit * (1 - 2 * lax.rem(lax.div(value, bit), 2))
        bit *= 2
    return value


def exchange_plan(grp_bits, x_bits):
    grp = [1 << b for b in reversed(range(grp_bits))]
    xs = [1 << (grp_bits + b) for b in reversed(range(x_bits))]
    half = grp_bits // 2
    orders = (grp[:1] + xs + grp[1:], grp[:1] + grp[-half:] + grp[1 : len(grp) - half] + xs)
    free = {}
    events = [(0.0, 0, 0), (0.0, 1, 0)]
    sequence = []
    while events:
        now, part, slot = heapq.heappop(events)
        order = orders[part]
        last = max([order.index(d) for d in order if d & slot], default=-1)
        onward = order[last + 1 :]
        sequence.append((part, slot, onward))
        for dim in onward:
            begin = max(now, free.get(dim, 0.0))
            free[dim] = begin + 2.6
            heapq.heappush(events, (begin + 3.6, part, slot ^ dim))
    return sequence


def sketch_kernel(
    fronts, leaves, c_ref, omega_ref, out_ref, cols, slots, acc, partial, local_sem, csend, crecv, send, recv, psem
):
    core = lax.rem(lax.axis_index("front"), 2)
    x_at = lax.div(lax.axis_index("front"), 2)
    grp_at = lax.axis_index("grp")
    x_count = fronts // 2
    grp_bits, x_bits = bits_of(leaves), bits_of(x_count)
    depth = omega_ref.shape[0]
    half = depth // 2
    rows = c_ref.shape[0]
    span = leaves * depth
    sibling = (x_at * 2 + 1 - core, grp_at)

    def partner(dim):
        if dim < leaves:
            return (x_at * 2 + core, flip(grp_at, dim))
        return (flip(x_at, dim // leaves) * 2 + core, grp_at)

    barrier = pltpu.get_barrier_semaphore()
    others = [partner(1 << b) for b in range(grp_bits + x_bits)] + [sibling]
    for other in others:
        pl.semaphore_signal(barrier, inc=1, device_id=other, device_id_type=MESH)
    mine = []
    for x in range(x_count):
        begin = pl.multiple_of((x * 2 + core) * span, 128)
        copy = pltpu.make_async_copy(
            c_ref.at[:, pl.ds(begin, span)], cols.at[0, :, pl.ds(x * span, span)], local_sem.at[x]
        )
        copy.start()
        mine.append(copy)
    pl.semaphore_wait(barrier, len(others))

    def piece(ref, part):
        return ref.at[pl.ds(part * half, half), :]

    def start(part, slot, dim):
        source = omega_ref if slot == 0 else slots.at[slot]
        copy = pltpu.make_async_remote_copy(
            src_ref=piece(source, part),
            dst_ref=piece(slots.at[slot ^ dim], part),
            send_sem=send.at[part, slot ^ dim],
            recv_sem=recv.at[part, slot ^ dim],
            device_id=partner(dim),
            device_id_type=MESH,
        )
        copy.start()
        return copy

    sequence = exchange_plan(grp_bits, x_bits)
    arrivals = {}
    given = []
    for part, slot, onward in sequence:
        if slot == 0:
            for dim in onward:
                arrivals[part, dim] = start(part, slot, dim)
    for x in range(x_count):
        begin = pl.multiple_of((x * 2 + 1 - core) * span, 128)
        copy = pltpu.make_async_remote_copy(
            src_ref=c_ref.at[:, pl.ds(begin, span)],
            dst_ref=cols.at[1, :, pl.ds(x * span, span)],
            send_sem=csend.at[x],
            recv_sem=crecv.at[x],
            device_id=sibling,
            device_id_type=MESH,
        )
        copy.start()
        given.append(copy)

    acc[...] = jnp.zeros_like(acc)
    ready = False
    waiting = []

    def multiply(part, slot):
        x_from = flip(x_at, slot // leaves)
        grp_from = flip(grp_at, slot % leaves)
        begin = pl.multiple_of((x_from * leaves + grp_from) * depth + part * half, 128)
        left = cols[:, :, pl.ds(begin, half)].reshape(2 * rows, half)
        source = omega_ref if slot == 0 else slots.at[slot]
        right = source[pl.ds(part * half, half), :]
        acc[...] += jnp.dot(left, right, preferred_element_type=jnp.float32)

    for number, (part, slot, onward) in enumerate(sequence):
        if slot != 0:
            arrivals[part, slot].wait_recv()
            for dim in onward:
                arrivals[part, slot ^ dim] = start(part, slot, dim)
        waiting.append((part, slot))
        if number >= 6 or number == len(sequence) - 1:
            if not ready:
                for copy in mine:
                    copy.wait()
                for copy in given:
                    copy.wait_recv()
                ready = True
            for item in waiting:
                multiply(*item)
            waiting = []

    final = pltpu.make_async_remote_copy(
        src_ref=acc.at[pl.ds(rows, rows), :],
        dst_ref=partial,
        send_sem=psem.at[0],
        recv_sem=psem.at[1],
        device_id=sibling,
        device_id_type=MESH,
    )
    final.start()
    for copy in given:
        copy.wait_send()
    for copy in arrivals.values():
        copy.wait_send()
    final.wait()
    out_ref[...] = (acc[pl.ds(0, rows), :] + partial[...]).astype(out_ref.dtype)


def make_sketch(contributions, omega):
    fronts, leaves = lax.axis_size("front"), lax.axis_size("grp")
    rows, order = contributions.shape
    depth, width = omega.shape
    count = fronts * leaves // 2
    return pl.pallas_call(
        functools.partial(sketch_kernel, fronts, leaves),
        out_shape=jax.ShapeDtypeStruct((rows, width), jnp.bfloat16),
        in_specs=[pl.BlockSpec(memory_space=pl.ANY), pl.BlockSpec(memory_space=pltpu.VMEM)],
        out_specs=pl.BlockSpec(memory_space=pltpu.VMEM),
        scratch_shapes=[
            pltpu.VMEM((2, rows, order // 2), jnp.bfloat16),
            pltpu.VMEM((count, depth, width), jnp.bfloat16),
            pltpu.VMEM((2 * rows, width), jnp.float32),
            pltpu.VMEM((rows, width), jnp.float32),
            pltpu.SemaphoreType.DMA((fronts // 2,)),
            pltpu.SemaphoreType.DMA((fronts // 2,)),
            pltpu.SemaphoreType.DMA((fronts // 2,)),
            pltpu.SemaphoreType.DMA((2, count)),
            pltpu.SemaphoreType.DMA((2, count)),
            pltpu.SemaphoreType.DMA((2,)),
        ],
        compiler_params=pltpu.CompilerParams(
            collective_id=0, has_side_effects=True, vmem_limit_bytes=40 * 2**20
        ),
        cost_estimate=pl.CostEstimate(
            flops=2 * rows * order * width, bytes_accessed=2 * rows * order, transcendentals=0
        ),
    )(contributions, omega)


def split(value):
    high = value.astype(jnp.bfloat16)
    return high, (value - high.astype(jnp.float32)).astype(jnp.bfloat16)


def halves(value):
    width = value.shape[1] // 2
    return value[:, :width] + value[:, width:]


def split_dot(left, right):
    lh, ll = split(left)
    rh, rl = split(right)
    both = jnp.concatenate([lh, ll], axis=1)
    top = jnp.concatenate([rh, rl], axis=1)
    low = jnp.concatenate([rh, jnp.zeros_like(rl)], axis=1)
    weights = jnp.concatenate([top, low], axis=0)
    return halves(jnp.dot(both, weights, preferred_element_type=jnp.float32))


def solve_kernel(arrived_ref, where_ref, basis_ref, stack_refs, pick_refs, leaf_ref, node_ref, state, gram_ref):
    bases = [basis_ref] + list(pick_refs)
    rank = basis_ref.shape[0]
    row = lax.broadcasted_iota(jnp.int32, (rank, rank), 0)
    col = lax.broadcasted_iota(jnp.int32, (rank, rank), 1)
    ident = (row == col).astype(jnp.float32)
    for at, ref in enumerate(bases):
        basis = ref[...]
        gram = lax.dot_general(
            basis, basis, (((1,), (1,)), ((), ())), precision=HIGHEST, preferred_element_type=jnp.float32
        )
        shift = 0.1 * (jnp.sum(gram * ident, keepdims=True) / rank) + 1e-05
        gram = gram + shift * ident
        scale = 1.0 / jnp.sum(gram * ident, keepdims=True)
        gram_ref[at] = gram
        rest = ident - gram * scale
        state[at, pl.ds(0, rank), :] = (ident + rest) * scale
        state[at, pl.ds(rank, rank), :] = split_dot(rest, rest)

    def step(_, carry):
        for at in range(len(bases)):
            now = state[at]
            grown = split_dot(now, now[rank:])
            state[at, pl.ds(0, rank), :] = now[:rank] + grown[:rank]
            state[at, pl.ds(rank, rank), :] = grown[rank:]
        return carry

    lax.fori_loop(0, STEPS - EXACT_STEPS - 1, step, 0)
    approx = [state[at, pl.ds(0, rank), :] for at in range(len(bases))]
    for _ in range(EXACT_STEPS):
        inner = [
            2.0 * ident - jnp.dot(gram_ref[at], approx[at], precision=HIGHEST, preferred_element_type=jnp.float32)
            for at in range(len(bases))
        ]
        approx = [
            jnp.dot(approx[at], inner[at], precision=HIGHEST, preferred_element_type=jnp.float32)
            for at in range(len(bases))
        ]
    lifted = [
        jnp.dot(jnp.transpose(ref[...]), approx[at], precision=HIGHEST, preferred_element_type=jnp.float32)
        for at, ref in enumerate(bases)
    ]
    spread = jnp.concatenate(split(lifted[0]), axis=1)
    small = halves(jnp.dot(arrived_ref[...], spread, preferred_element_type=jnp.float32))
    small = jnp.concatenate(split(small), axis=1)
    slots = arrived_ref.shape[0]
    adding = (
        lax.broadcasted_iota(jnp.int32, (leaf_ref.shape[0], slots), 0) == where_ref[...]
    ).astype(jnp.float32).astype(jnp.bfloat16)
    leaf_ref[...] = halves(jnp.dot(adding, small, preferred_element_type=jnp.float32))
    for level, ref in enumerate(stack_refs):
        node_ref[level] = split_dot(ref[...], lifted[level + 1])


def solve_all(arrived, where_to, basis, stacks, picks):
    rank = basis.shape[0]
    vmem = pl.BlockSpec(memory_space=pltpu.VMEM)
    levels = len(stacks)
    return pl.pallas_call(
        solve_kernel,
        out_shape=(
            jax.ShapeDtypeStruct((PR_DEV, rank), jnp.float32),
            jax.ShapeDtypeStruct((levels, 2 * rank, rank), jnp.float32),
        ),
        in_specs=[vmem, vmem, vmem, [vmem] * levels, [vmem] * levels],
        out_specs=(vmem, vmem),
        scratch_shapes=[
            pltpu.VMEM((levels + 1, 2 * rank, rank), jnp.float32),
            pltpu.VMEM((levels + 1, rank, rank), jnp.float32),
        ],
        compiler_params=pltpu.CompilerParams(vmem_limit_bytes=40 * 2**20),
    )(arrived, where_to, basis, stacks, picks)


def from_partner(block, axis, stride):
    count = lax.axis_size(axis)
    route = []
    for low in range(count):
        high = low | 1 << stride
        if high != low and high < count:
            route += [(low, high), (high, low)]
    return lax.ppermute(block, axis, route)


def select_rows(rows, index):
    picker = (index[:, None] == jnp.arange(rows.shape[0], dtype=jnp.int32)[None, :]).astype(
        jnp.float32
    )
    return jnp.dot(picker, rows, precision=HIGHEST)


def local(
    contributions,
    sketch_matrix,
    destinations,
    parent_rows,
    front_sizes,
    leaf_skeleton,
    merge_skeleton,
):
    fronts = lax.axis_size("front")
    leaves = lax.axis_size("grp")
    devices = fronts * leaves
    grp_index = lax.axis_index("grp")
    myself = lax.axis_index("front") * leaves + grp_index
    rows_dev = contributions.shape[0]
    width = sketch_matrix.shape[1]
    capacity = 2 * rows_dev // devices
    sketch = make_sketch(contributions, sketch_matrix)
    every_dest = destinations[:, 0].reshape(devices, rows_dev)
    every_row = parent_rows.reshape(devices, rows_dev)
    mine = lax.dynamic_index_in_dim(every_dest, myself, 0, keepdims=False)
    owners = jnp.arange(devices, dtype=jnp.int32)
    hits = (mine[:, None] == owners[None, :]).astype(jnp.int32)
    before = jnp.cumsum(hits, axis=0) - hits
    slot_of = jnp.sum(before * hits, axis=1)
    keys = mine * capacity + slot_of
    placing = (keys[None, :] == jnp.arange(devices * capacity, dtype=jnp.int32)[:, None]).astype(
        jnp.bfloat16
    )
    packed = jnp.dot(placing, sketch, preferred_element_type=jnp.float32).astype(jnp.bfloat16)
    packed = packed.reshape(devices, capacity, width)
    arrived = lax.all_to_all(
        packed, ("front", "grp"), split_axis=0, concat_axis=0, tiled=True
    ).reshape(devices * capacity, width)
    landing = (every_dest == myself).astype(jnp.int32)
    slots = jnp.cumsum(landing, axis=1) - landing
    match = landing[:, None, :] * (
        slots[:, None, :] == jnp.arange(capacity, dtype=jnp.int32)[None, :, None]
    ).astype(jnp.int32)
    local_row = jnp.sum(match * every_row[:, None, :], axis=2)
    filled = jnp.sum(match, axis=2)
    live = (filled > 0) & (grp_index * PR_DEV + local_row < front_sizes[0])
    where_to = jnp.where(live, local_row, -1).reshape(1, devices * capacity)
    chosen = (leaf_skeleton[0, 0][:, None] == where_to).astype(jnp.bfloat16)
    basis = jnp.dot(chosen, arrived, preferred_element_type=jnp.float32)
    skeletons = merge_skeleton[0]
    stacks, picks = [], []
    current = basis
    for level in range(LEVELS):
        partner = from_partner(current, "grp", level)
        upper_side = grp_index >> level & 1 == 1
        first = jnp.where(upper_side, partner, current)
        second = jnp.where(upper_side, current, partner)
        stacked = jnp.concatenate([first, second], axis=0)
        node = leaves - (leaves >> level) + (grp_index >> level + 1)
        index = lax.dynamic_index_in_dim(skeletons, node, 0, keepdims=False)
        current = select_rows(stacked, index)
        stacks.append(stacked)
        picks.append(current)
    leaf_map, node_maps = solve_all(arrived, where_to, basis, stacks, picks)
    return (leaf_map[None], node_maps[None, None], current[None, None])


def solution(mesh):
    in_specs = (
        P(("front", "grp"), None),
        P(("front", "grp"), None),
        P(),
        P(),
        P("front"),
        P("front", "grp", None),
        P("front", None, None),
    )
    out_specs = (
        P("front", "grp", None),
        P("front", "grp", None, None, None),
        P("front", "grp", None, None),
    )
    return jax.shard_map(local, mesh=mesh, in_specs=in_specs, out_specs=out_specs, check_vma=False)
```

```python
import functools
import heapq

import jax
import jax.numpy as jnp
from jax import lax
from jax.experimental import pallas as pl
from jax.experimental.pallas import tpu as pltpu
from jax.sharding import PartitionSpec as P

PR_DEV = 1024
LEVELS = 3
STEPS = 24
EXACT_STEPS = 2
CUTS = 4
HIGHEST = lax.Precision.HIGHEST
MESH = pl.DeviceIdType.MESH


def bits_of(count):
    return count.bit_length() - 1


def flip(value, mask):
    bit = 1
    while bit <= mask:
        if mask & bit:
            value = value + bit * (1 - 2 * lax.rem(lax.div(value, bit), 2))
        bit *= 2
    return value


def exchange_plan(grp_bits, x_bits, cuts):
    grp = [1 << b for b in reversed(range(grp_bits))]
    xs = [1 << (grp_bits + b) for b in reversed(range(x_bits))]
    half = grp_bits // 2
    near = grp[-half:]
    orders = (grp[:1] + xs + grp[1:], grp[:1] + near + grp[1 : len(grp) - half] + xs)
    link = {d: "x" if d in xs else "near" if d in near else "far" for d in grp + xs}
    free = {}
    events = [(0.0, part, 0) for part in range(cuts)]
    sequence = []
    while events:
        now, part, slot = heapq.heappop(events)
        order = orders[part % 2]
        last = max([order.index(d) for d in order if d & slot], default=-1)
        onward = order[last + 1 :]
        sequence.append((part, slot, onward))
        for dim in onward:
            begin = max(now, free.get(link[dim], 0.0))
            free[link[dim]] = begin + 1.0
            heapq.heappush(events, (begin + 1.0 + 0.2 * cuts, part, slot ^ dim))
    return sequence


def split(value):
    high = value.astype(jnp.bfloat16)
    return high, (value - high.astype(jnp.float32)).astype(jnp.bfloat16)


def halves(value):
    width = value.shape[1] // 2
    return value[:, :width] + value[:, width:]


def split_dot(left, right):
    lh, ll = split(left)
    rh, rl = split(right)
    both = jnp.concatenate([lh, ll], axis=1)
    top = jnp.concatenate([rh, rl], axis=1)
    low = jnp.concatenate([rh, jnp.zeros_like(rl)], axis=1)
    weights = jnp.concatenate([top, low], axis=0)
    return halves(jnp.dot(both, weights, preferred_element_type=jnp.float32))


def full_dot(left, right):
    return jnp.dot(left, right, precision=HIGHEST, preferred_element_type=jnp.float32)


def take_rows(picker, rows):
    width = rows.shape[1]
    high, rest = split(rows)
    rest = rows - high.astype(jnp.float32)
    middle, low = split(rest)
    parts = jnp.concatenate([high, middle, low], axis=1)
    found = jnp.dot(picker, parts, preferred_element_type=jnp.float32)
    return (found[:, :width] + found[:, width : 2 * width]) + found[:, 2 * width :]


def as_bf16(condition):
    return condition.astype(jnp.float32).astype(jnp.bfloat16)


def column_of(line):
    return jnp.transpose(jnp.broadcast_to(line.astype(jnp.float32), (128, line.shape[1])))


def whole_kernel(
    fronts, leaves, capacity,
    c_ref, omega_ref, dest_ref, prow_ref, size_ref, leafskel_ref, mergeskel_ref,
    leaf_ref, node_ref, top_ref,
    cols, slots, acc, partial, packed, arrived, stacks, bases, grams, state,
    local_sem, csend, crecv, send, recv, psem, asend, arecv, lsend, lrecv,
):
    front_at = lax.axis_index("front")
    grp_at = lax.axis_index("grp")
    core = lax.rem(front_at, 2)
    x_at = lax.div(front_at, 2)
    devices = fronts * leaves
    myself = front_at * leaves + grp_at
    x_count = fronts // 2
    grp_bits, x_bits = bits_of(leaves), bits_of(x_count)
    depth = omega_ref.shape[0]
    cut = depth // CUTS
    rows, width = c_ref.shape[0], omega_ref.shape[1]
    span = leaves * depth
    rank = leafskel_ref.shape[1]
    sibling = (x_at * 2 + 1 - core, grp_at)

    def device(number):
        return (lax.div(number, leaves), lax.rem(number, leaves))

    def partner(dim):
        if dim < leaves:
            return (front_at, flip(grp_at, dim))
        return (flip(x_at, dim // leaves) * 2 + core, grp_at)

    barrier = pltpu.get_barrier_semaphore()

    def greet(step, carry):
        other = device(lax.rem(myself + step, devices))
        pl.semaphore_signal(barrier, inc=1, device_id=other, device_id_type=MESH)
        return carry

    lax.fori_loop(1, devices, greet, 0)
    mine = []
    for x in range(x_count):
        begin = pl.multiple_of((x * 2 + core) * span, 128)
        copy = pltpu.make_async_copy(
            c_ref.at[:, pl.ds(begin, span)], cols.at[0, :, pl.ds(x * span, span)], local_sem.at[x]
        )
        copy.start()
        mine.append(copy)
    pl.semaphore_wait(barrier, devices - 1)

    def start(part, slot, dim):
        source = omega_ref if slot == 0 else slots.at[slot]
        copy = pltpu.make_async_remote_copy(
            src_ref=source.at[pl.ds(part * cut, cut), :],
            dst_ref=slots.at[slot ^ dim, pl.ds(part * cut, cut), :],
            send_sem=send.at[part, slot ^ dim],
            recv_sem=recv.at[part, slot ^ dim],
            device_id=partner(dim),
            device_id_type=MESH,
        )
        copy.start()
        return copy

    sequence = exchange_plan(grp_bits, x_bits, CUTS)
    arrivals = {}
    given = []
    for part, slot, onward in sequence:
        if slot == 0:
            for dim in onward:
                arrivals[part, dim] = start(part, slot, dim)
    for x in range(x_count):
        begin = pl.multiple_of((x * 2 + 1 - core) * span, 128)
        copy = pltpu.make_async_remote_copy(
            src_ref=c_ref.at[:, pl.ds(begin, span)],
            dst_ref=cols.at[1, :, pl.ds(x * span, span)],
            send_sem=csend.at[x],
            recv_sem=crecv.at[x],
            device_id=sibling,
            device_id_type=MESH,
        )
        copy.start()
        given.append(copy)

    acc[...] = jnp.zeros_like(acc)

    chunks = width // 128
    used = capacity * chunks
    lines = packed.shape[1]
    shape = (devices, lines, rows)
    block_at = lax.broadcasted_iota(jnp.int32, shape, 0).astype(jnp.float32)
    line_at = lax.broadcasted_iota(jnp.int32, shape, 1)
    slot_at = jnp.where(line_at < used, lax.rem(line_at, capacity), -1).astype(jnp.float32)
    row = lax.broadcasted_iota(jnp.int32, (rows, rows), 0)
    col = lax.broadcasted_iota(jnp.int32, (rows, rows), 1)
    going = dest_ref[pl.ds(myself, 1), :].astype(jnp.float32)
    same = (column_of(going)[:, :rows] == going) & (row < col)
    rank_in = jnp.sum(same.astype(jnp.float32), axis=0, keepdims=True)
    placing = as_bf16((block_at == going.reshape(1, 1, rows)) & (slot_at == rank_in.reshape(1, 1, rows)))
    placing = placing.reshape(devices * lines, rows)

    coming = dest_ref[...] == myself
    ahead = jnp.dot(as_bf16(coming), as_bf16(row < col), preferred_element_type=jnp.float32)
    ahead = jnp.where(coming, ahead, -2.0)
    live = prow_ref[...] + grp_at * PR_DEV < size_ref[...]
    landing = jnp.where(live, prow_ref[...] + 1, 0).astype(jnp.float32)
    hit = ahead.reshape(devices, 1, rows) == slot_at
    where_to = jnp.sum(jnp.where(hit, landing.reshape(devices, 1, rows), 0.0), axis=2, keepdims=True) - 1.0
    where_to = where_to.reshape(devices * lines, 1)
    where_to = jnp.transpose(jnp.broadcast_to(where_to, (devices * lines, 128)))[0:1, :]
    chosen = as_bf16(column_of(leafskel_ref[...])[:, 0:1] == where_to)
    picks = []
    for level in range(LEVELS):
        node = leaves - leaves // 2**level + lax.div(grp_at, 2 ** (level + 1))
        wanted = column_of(mergeskel_ref[pl.ds(node, 1), :])[:, 0:1]
        at = lax.broadcasted_iota(jnp.int32, (rank, 2 * rank), 1).astype(jnp.float32)
        picks.append(as_bf16(wanted == at))

    def multiply(slot):
        x_from = flip(x_at, slot // leaves)
        grp_from = flip(grp_at, slot % leaves)
        begin = pl.multiple_of((x_from * leaves + grp_from) * depth, 128)
        left = cols[:, :, pl.ds(begin, depth)].reshape(2 * rows, depth)
        right = omega_ref[...] if slot == 0 else slots[slot]
        acc[...] += jnp.dot(left, right, preferred_element_type=jnp.float32)

    held = {}
    ready = False
    waiting = []
    for number, (part, slot, onward) in enumerate(sequence):
        if slot != 0:
            arrivals[part, slot].wait_recv()
            for dim in onward:
                arrivals[part, slot ^ dim] = start(part, slot, dim)
        held[slot] = held.get(slot, 0) + 1
        if held[slot] == CUTS:
            waiting.append(slot)
        if number >= len(sequence) // 4:
            if not ready:
                for copy in mine:
                    copy.wait()
                for copy in given:
                    copy.wait_recv()
                ready = True
            for item in waiting:
                multiply(item)
            waiting = []

    final = pltpu.make_async_remote_copy(
        src_ref=acc.at[pl.ds(rows, rows), :],
        dst_ref=partial,
        send_sem=psem.at[0],
        recv_sem=psem.at[1],
        device_id=sibling,
        device_id_type=MESH,
    )
    final.start()
    final.wait_recv()
    sketch = (acc[pl.ds(0, rows), :] + partial[...]).astype(jnp.bfloat16)

    placed = jnp.dot(placing, sketch, preferred_element_type=jnp.float32).reshape(devices, lines, width)
    line = lax.broadcasted_iota(jnp.int32, (devices, lines, 128), 1)
    chunk_at = lax.div(line, capacity)
    sent = placed[:, :, :128]
    for chunk in range(1, chunks):
        sent = jnp.where(chunk_at == chunk, placed[:, :, chunk * 128 : (chunk + 1) * 128], sent)
    packed[...] = sent.astype(jnp.bfloat16)

    def deliver(step):
        number = lax.rem(myself + step, devices)
        return pltpu.make_async_remote_copy(
            src_ref=packed.at[number],
            dst_ref=arrived.at[myself],
            send_sem=asend.at[step],
            recv_sem=arecv.at[step],
            device_id=device(number),
            device_id_type=MESH,
        )

    def deliver_start(step, carry):
        deliver(step).start()
        return carry

    lax.fori_loop(1, devices, deliver_start, 0)
    arrived[pl.ds(myself, 1)] = packed[pl.ds(myself, 1)]

    def deliver_wait(step, carry):
        number = lax.rem(myself + devices - step, devices)
        pltpu.make_async_remote_copy(
            src_ref=packed.at[number],
            dst_ref=arrived.at[number],
            send_sem=asend.at[step],
            recv_sem=arecv.at[step],
            device_id=device(number),
            device_id_type=MESH,
        ).wait_recv()
        return carry

    lax.fori_loop(1, devices, deliver_wait, 0)
    flat = arrived[...].astype(jnp.float32)
    wide = [jnp.where(chunk_at == chunk, flat, 0.0) for chunk in range(chunks)]
    landed = jnp.concatenate(wide, axis=2).reshape(devices * lines, width).astype(jnp.bfloat16)

    eye_row = lax.broadcasted_iota(jnp.int32, (rank, rank), 0)
    ident = (eye_row == lax.broadcasted_iota(jnp.int32, (rank, rank), 1)).astype(jnp.float32)

    def offer(level, basis):
        bases[level] = basis
        side = lax.rem(lax.div(grp_at, 2**level), 2)
        place = pl.ds(pl.multiple_of(side * rank, rank), rank)
        stacks[level, place, :] = basis
        copy = pltpu.make_async_remote_copy(
            src_ref=stacks.at[level, place, :],
            dst_ref=stacks.at[level, place, :],
            send_sem=lsend.at[level],
            recv_sem=lrecv.at[level],
            device_id=(front_at, flip(grp_at, 2**level)),
            device_id_type=MESH,
        )
        copy.start()
        return copy

    def begin_solve(at):
        basis = bases[at]
        gram = lax.dot_general(
            basis, basis, (((1,), (1,)), ((), ())), precision=HIGHEST, preferred_element_type=jnp.float32
        )
        shift = 0.1 * (jnp.sum(gram * ident, keepdims=True) / rank) + 1e-05
        gram = gram + shift * ident
        scale = 1.0 / jnp.sum(gram * ident, keepdims=True)
        grams[at] = gram
        rest = ident - gram * scale
        state[at, pl.ds(0, rank), :] = (ident + rest) * scale
        state[at, pl.ds(rank, rank), :] = split_dot(rest, rest)

    def advance(systems, count):
        def step(_, carry):
            for at in systems:
                now = state[at]
                grown = split_dot(now, now[rank:])
                state[at, pl.ds(0, rank), :] = now[:rank] + grown[:rank]
                state[at, pl.ds(rank, rank), :] = grown[rank:]
            return carry

        lax.fori_loop(0, count, step, 0)

    def lift(systems):
        approx = {at: state[at, pl.ds(0, rank), :] for at in systems}
        for _ in range(EXACT_STEPS):
            inner = {at: 2.0 * ident - full_dot(grams[at], approx[at]) for at in systems}
            approx = {at: full_dot(approx[at], inner[at]) for at in systems}
        return {at: full_dot(jnp.transpose(bases[at]), approx[at]) for at in systems}

    total = STEPS - EXACT_STEPS - 1
    early = total // 2
    late = total - early
    copy = offer(0, jnp.dot(chosen, landed, preferred_element_type=jnp.float32))
    copies = [copy]
    begin_solve(0)
    advance([0], early)
    for level in range(LEVELS):
        copies[level].wait_recv()
        basis = take_rows(picks[level], stacks[level])
        if level < LEVELS - 1:
            copies.append(offer(level + 1, basis))
        else:
            bases[LEVELS] = basis
            top_ref[...] = basis
        begin_solve(level + 1)
        advance([level, level + 1], late if level != 1 else early)
        if level == 0:
            lifted = lift([0])[0]
            small = halves(jnp.dot(landed, jnp.concatenate(split(lifted), axis=1), preferred_element_type=jnp.float32))
            small = jnp.concatenate(split(small), axis=1)
            spot = lax.broadcasted_iota(jnp.int32, (leaf_ref.shape[0], devices * lines), 0).astype(jnp.float32)
            leaf_ref[...] = halves(jnp.dot(as_bf16(spot == where_to), small, preferred_element_type=jnp.float32))
        if level == 1:
            pass
    advance([LEVELS], early)
    lifted = lift(list(range(1, LEVELS + 1)))
    for level in range(LEVELS):
        node_ref[level] = split_dot(stacks[level], lifted[level + 1])

    for copy in given + list(arrivals.values()) + [final] + copies:
        copy.wait_send()

    def deliver_end(step, carry):
        deliver(step).wait_send()
        return carry

    lax.fori_loop(1, devices, deliver_end, 0)


def local(
    contributions,
    sketch_matrix,
    destinations,
    parent_rows,
    front_sizes,
    leaf_skeleton,
    merge_skeleton,
):
    fronts, leaves = lax.axis_size("front"), lax.axis_size("grp")
    devices = fronts * leaves
    rows, order = contributions.shape
    depth, width = sketch_matrix.shape
    rank = leaf_skeleton.shape[-1]
    count = devices // 2
    capacity = 2 * rows // devices
    lines = -(-capacity * (width // 128) // 16) * 16
    vmem = pl.BlockSpec(memory_space=pltpu.VMEM)
    semaphores = [
        (fronts // 2,), (fronts // 2,), (fronts // 2,), (CUTS, count), (CUTS, count), (2,),
        (devices,), (devices,), (LEVELS,), (LEVELS,),
    ]
    leaf_map, node_maps, top_rows = pl.pallas_call(
        functools.partial(whole_kernel, fronts, leaves, capacity),
        out_shape=(
            jax.ShapeDtypeStruct((PR_DEV, rank), jnp.float32),
            jax.ShapeDtypeStruct((LEVELS, 2 * rank, rank), jnp.float32),
            jax.ShapeDtypeStruct((rank, width), jnp.float32),
        ),
        in_specs=[pl.BlockSpec(memory_space=pltpu.HBM)] + [vmem] * 6,
        out_specs=(vmem, vmem, vmem),
        scratch_shapes=[
            pltpu.VMEM((2, rows, order // 2), jnp.bfloat16),
            pltpu.VMEM((count, depth, width), jnp.bfloat16),
            pltpu.VMEM((2 * rows, width), jnp.float32),
            pltpu.VMEM((rows, width), jnp.float32),
            pltpu.VMEM((devices, lines, 128), jnp.bfloat16),
            pltpu.VMEM((devices, lines, 128), jnp.bfloat16),
            pltpu.VMEM((LEVELS, 2 * rank, width), jnp.float32),
            pltpu.VMEM((LEVELS + 1, rank, width), jnp.float32),
            pltpu.VMEM((LEVELS + 1, rank, rank), jnp.float32),
            pltpu.VMEM((LEVELS + 1, 2 * rank, rank), jnp.float32),
        ]
        + [pltpu.SemaphoreType.DMA(shape) for shape in semaphores],
        compiler_params=pltpu.CompilerParams(
            collective_id=0, has_side_effects=True, vmem_limit_bytes=40 * 2**20
        ),
        cost_estimate=pl.CostEstimate(
            flops=2 * rows * order * width, bytes_accessed=2 * rows * order, transcendentals=0
        ),
    )(
        contributions,
        sketch_matrix,
        destinations.reshape(devices, rows),
        parent_rows.reshape(devices, rows),
        jnp.broadcast_to(front_sizes[None, :], (1, rows)),
        leaf_skeleton[0],
        merge_skeleton[0],
    )
    return (leaf_map[None], node_maps[None, None], top_rows[None, None])


def solution(mesh):
    in_specs = (
        P(("front", "grp"), None),
        P(("front", "grp"), None),
        P(),
        P(),
        P("front"),
        P("front", "grp", None),
        P("front", None, None),
    )
    out_specs = (
        P("front", "grp", None),
        P("front", "grp", None, None, None),
        P("front", "grp", None, None),
    )
    return jax.shard_map(local, mesh=mesh, in_specs=in_specs, out_specs=out_specs, check_vma=False)
```

```python
import functools
import heapq

import jax
import jax.numpy as jnp
from jax import lax
from jax.experimental import pallas as pl
from jax.experimental.pallas import tpu as pltpu
from jax.sharding import PartitionSpec as P

PR_DEV = 1024
LEVELS = 3
STEPS = 24
EXACT_STEPS = 1
CUTS = 4
HIGHEST = lax.Precision.HIGHEST
MESH = pl.DeviceIdType.MESH


def bits_of(count):
    return count.bit_length() - 1


def flip(value, mask):
    bit = 1
    while bit <= mask:
        if mask & bit:
            value = value + bit * (1 - 2 * lax.rem(lax.div(value, bit), 2))
        bit *= 2
    return value


def exchange_plan(grp_bits, x_bits, cuts):
    grp = [1 << b for b in reversed(range(grp_bits))]
    xs = [1 << (grp_bits + b) for b in reversed(range(x_bits))]
    half = grp_bits // 2
    near = grp[-half:]
    orders = (grp[:1] + xs + grp[1:], grp[:1] + near + grp[1 : len(grp) - half] + xs)
    link = {d: "x" if d in xs else "near" if d in near else "far" for d in grp + xs}
    free = {}
    events = [(0.0, part, 0) for part in range(cuts)]
    sequence = []
    while events:
        now, part, slot = heapq.heappop(events)
        order = orders[part % 2]
        last = max([order.index(d) for d in order if d & slot], default=-1)
        onward = order[last + 1 :]
        sequence.append((part, slot, onward))
        for dim in onward:
            begin = max(now, free.get(link[dim], 0.0))
            free[link[dim]] = begin + 1.0
            heapq.heappush(events, (begin + 1.0 + 0.2 * cuts, part, slot ^ dim))
    return sequence


def split(value):
    high = value.astype(jnp.bfloat16)
    return high, (value - high.astype(jnp.float32)).astype(jnp.bfloat16)


def halves(value):
    width = value.shape[1] // 2
    return value[:, :width] + value[:, width:]


def split_dot(left, right):
    lh, ll = split(left)
    rh, rl = split(right)
    both = jnp.concatenate([lh, ll], axis=1)
    top = jnp.concatenate([rh, rl], axis=1)
    low = jnp.concatenate([rh, jnp.zeros_like(rl)], axis=1)
    weights = jnp.concatenate([top, low], axis=0)
    return halves(jnp.dot(both, weights, preferred_element_type=jnp.float32))


def full_dot(left, right):
    return jnp.dot(left, right, precision=HIGHEST, preferred_element_type=jnp.float32)


def take_rows(picker, rows):
    width = rows.shape[1]
    high, rest = split(rows)
    rest = rows - high.astype(jnp.float32)
    middle, low = split(rest)
    parts = jnp.concatenate([high, middle, low], axis=1)
    found = jnp.dot(picker, parts, preferred_element_type=jnp.float32)
    return (found[:, :width] + found[:, width : 2 * width]) + found[:, 2 * width :]


def as_bf16(condition):
    return condition.astype(jnp.float32).astype(jnp.bfloat16)


def column_of(line):
    return jnp.transpose(jnp.broadcast_to(line.astype(jnp.float32), (128, line.shape[1])))


def whole_kernel(
    fronts, leaves, capacity,
    c_ref, omega_ref, dest_hbm, prow_hbm, size_hbm, leafskel_hbm, mergeskel_hbm,
    leaf_hbm, node_hbm, top_hbm,
    dest_ref, prow_ref, size_ref, leafskel_ref, mergeskel_ref, leaf_ref, node_ref,
    cols, slots, acc, partial, packed, arrived, stacks, bases, grams, state,
    local_sem, table_sem, out_sem, csend, crecv, send, recv, psem, asend, arecv, lsend, lrecv,
):
    front_at = lax.axis_index("front")
    grp_at = lax.axis_index("grp")
    core = lax.rem(front_at, 2)
    x_at = lax.div(front_at, 2)
    devices = fronts * leaves
    myself = front_at * leaves + grp_at
    x_count = fronts // 2
    grp_bits, x_bits = bits_of(leaves), bits_of(x_count)
    depth = omega_ref.shape[0]
    cut = depth // CUTS
    rows, width = c_ref.shape[0], omega_ref.shape[1]
    span = leaves * depth
    rank = leafskel_ref.shape[1]
    sibling = (x_at * 2 + 1 - core, grp_at)

    def device(number):
        return (lax.div(number, leaves), lax.rem(number, leaves))

    def partner(dim):
        if dim < leaves:
            return (front_at, flip(grp_at, dim))
        return (flip(x_at, dim // leaves) * 2 + core, grp_at)

    tables = [
        (dest_hbm, dest_ref), (prow_hbm, prow_ref), (size_hbm, size_ref),
        (leafskel_hbm, leafskel_ref), (mergeskel_hbm, mergeskel_ref),
    ]
    tables = [pltpu.make_async_copy(a, b, table_sem.at[at]) for at, (a, b) in enumerate(tables)]
    barrier = pltpu.get_barrier_semaphore()

    def greet(step, carry):
        other = device(lax.rem(myself + step, devices))
        pl.semaphore_signal(barrier, inc=1, device_id=other, device_id_type=MESH)
        return carry

    lax.fori_loop(1, devices, greet, 0)
    mine = []
    for x in range(x_count):
        begin = pl.multiple_of((x * 2 + core) * span, 128)
        copy = pltpu.make_async_copy(
            c_ref.at[:, pl.ds(begin, span)], cols.at[0, :, pl.ds(x * span, span)], local_sem.at[x]
        )
        copy.start()
        mine.append(copy)
    copy = pltpu.make_async_copy(omega_ref, slots.at[0], local_sem.at[x_count])
    copy.start()
    mine.append(copy)
    for copy in tables:
        copy.start()
    pl.semaphore_wait(barrier, devices - 1)

    def start(part, slot, dim):
        source = omega_ref if slot == 0 else slots.at[slot]
        copy = pltpu.make_async_remote_copy(
            src_ref=source.at[pl.ds(part * cut, cut), :],
            dst_ref=slots.at[slot ^ dim, pl.ds(part * cut, cut), :],
            send_sem=send.at[part, slot ^ dim],
            recv_sem=recv.at[part, slot ^ dim],
            device_id=partner(dim),
            device_id_type=MESH,
        )
        copy.start()
        return copy

    sequence = exchange_plan(grp_bits, x_bits, CUTS)
    arrivals = {}
    given = []
    for part, slot, onward in sequence:
        if slot == 0:
            for dim in onward:
                arrivals[part, dim] = start(part, slot, dim)
    for x in range(x_count):
        begin = pl.multiple_of((x * 2 + 1 - core) * span, 128)
        copy = pltpu.make_async_remote_copy(
            src_ref=c_ref.at[:, pl.ds(begin, span)],
            dst_ref=cols.at[1, :, pl.ds(x * span, span)],
            send_sem=csend.at[x],
            recv_sem=crecv.at[x],
            device_id=sibling,
            device_id_type=MESH,
        )
        copy.start()
        given.append(copy)

    acc[...] = jnp.zeros_like(acc)

    chunks = width // 128
    used = capacity * chunks
    lines = packed.shape[1]
    kept = capacity if capacity % 8 == 0 else lines

    def make_tables():
        for copy in tables:
            copy.wait()
        shape = (devices, lines, rows)
        block_at = lax.broadcasted_iota(jnp.int32, shape, 0).astype(jnp.float32)
        line_at = lax.broadcasted_iota(jnp.int32, shape, 1)
        slot_at = jnp.where(line_at < used, lax.rem(line_at, capacity), -1).astype(jnp.float32)
        row = lax.broadcasted_iota(jnp.int32, (rows, rows), 0)
        col = lax.broadcasted_iota(jnp.int32, (rows, rows), 1)
        going = dest_ref[pl.ds(myself, 1), :].astype(jnp.float32)
        same = (column_of(going)[:, :rows] == going) & (row < col)
        rank_in = jnp.sum(same.astype(jnp.float32), axis=0, keepdims=True)
        placing = as_bf16((block_at == going.reshape(1, 1, rows)) & (slot_at == rank_in.reshape(1, 1, rows)))
        placing = placing.reshape(devices * lines, rows)

        coming = dest_ref[...] == myself
        ahead = jnp.dot(as_bf16(coming), as_bf16(row < col), preferred_element_type=jnp.float32)
        ahead = jnp.where(coming, ahead, -2.0)
        live = prow_ref[...] + grp_at * PR_DEV < size_ref[...]
        landing = jnp.where(live, prow_ref[...] + 1, 0).astype(jnp.float32)
        hit = ahead.reshape(devices, 1, rows) == slot_at[:, :kept, :]
        where_to = jnp.sum(jnp.where(hit, landing.reshape(devices, 1, rows), 0.0), axis=2, keepdims=True) - 1.0
        where_to = where_to.reshape(devices * kept, 1)
        where_to = jnp.transpose(jnp.broadcast_to(where_to, (devices * kept, 128)))[0:1, :]
        chosen = as_bf16(column_of(leafskel_ref[...])[:, 0:1] == where_to)
        picks = []
        for level in range(LEVELS):
            node = leaves - leaves // 2**level + lax.div(grp_at, 2 ** (level + 1))
            wanted = column_of(mergeskel_ref[node])[:, 0:1]
            at = lax.broadcasted_iota(jnp.int32, (rank, 2 * rank), 1).astype(jnp.float32)
            picks.append(as_bf16(wanted == at))
        return placing, where_to, chosen, picks

    def multiply(slot):
        x_from = flip(x_at, slot // leaves)
        grp_from = flip(grp_at, slot % leaves)
        begin = pl.multiple_of((x_from * leaves + grp_from) * depth, 128)
        left = cols[:, :, pl.ds(begin, depth)].reshape(2 * rows, depth)
        acc[...] += jnp.dot(left, slots[slot], preferred_element_type=jnp.float32)

    held = {}
    forwards = max(at for at, item in enumerate(sequence) if item[2])
    ready = False
    waiting = []
    for number, (part, slot, onward) in enumerate(sequence):
        if slot != 0:
            arrivals[part, slot].wait_recv()
            for dim in onward:
                arrivals[part, slot ^ dim] = start(part, slot, dim)
        held[slot] = held.get(slot, 0) + 1
        if held[slot] == CUTS:
            waiting.append(slot)
        if number >= len(sequence) // 4:
            if not ready:
                for copy in mine:
                    copy.wait()
                for copy in given:
                    copy.wait_recv()
                ready = True
            if waiting:
                multiply(waiting.pop(0))
        if number == forwards:
            placing, where_to, chosen, picks = make_tables()
    for item in waiting:
        multiply(item)

    final = pltpu.make_async_remote_copy(
        src_ref=acc.at[pl.ds(rows, rows), :],
        dst_ref=partial,
        send_sem=psem.at[0],
        recv_sem=psem.at[1],
        device_id=sibling,
        device_id_type=MESH,
    )
    final.start()
    final.wait_recv()
    sketch = (acc[pl.ds(0, rows), :] + partial[...]).astype(jnp.bfloat16)

    placed = jnp.dot(placing, sketch, preferred_element_type=jnp.float32).reshape(devices, lines, width)
    line = lax.broadcasted_iota(jnp.int32, (devices, lines, 128), 1)
    chunk_at = lax.div(line, capacity)
    sent = placed[:, :, :128]
    for chunk in range(1, chunks):
        sent = jnp.where(chunk_at == chunk, placed[:, :, chunk * 128 : (chunk + 1) * 128], sent)
    packed[...] = sent.astype(jnp.bfloat16)

    def deliver(step):
        number = lax.rem(myself + step, devices)
        return pltpu.make_async_remote_copy(
            src_ref=packed.at[number],
            dst_ref=arrived.at[myself],
            send_sem=asend.at[step],
            recv_sem=arecv.at[step],
            device_id=device(number),
            device_id_type=MESH,
        )

    def deliver_start(step, carry):
        deliver(step).start()
        return carry

    lax.fori_loop(1, devices, deliver_start, 0)
    arrived[pl.ds(myself, 1)] = packed[pl.ds(myself, 1)]

    def deliver_wait(step, carry):
        number = lax.rem(myself + devices - step, devices)
        pltpu.make_async_remote_copy(
            src_ref=packed.at[number],
            dst_ref=arrived.at[number],
            send_sem=asend.at[step],
            recv_sem=arecv.at[step],
            device_id=device(number),
            device_id_type=MESH,
        ).wait_recv()
        return carry

    lax.fori_loop(1, devices, deliver_wait, 0)
    flat = arrived[...].astype(jnp.float32)
    if kept == capacity:
        wide = [flat[:, chunk * capacity : (chunk + 1) * capacity] for chunk in range(chunks)]
    else:
        wide = [jnp.where(chunk_at == chunk, flat, 0.0) for chunk in range(chunks)]
    landed = jnp.concatenate(wide, axis=2).reshape(devices * kept, width).astype(jnp.bfloat16)

    eye_row = lax.broadcasted_iota(jnp.int32, (rank, rank), 0)
    ident = (eye_row == lax.broadcasted_iota(jnp.int32, (rank, rank), 1)).astype(jnp.float32)

    def offer(level, basis):
        bases[level] = basis
        side = lax.rem(lax.div(grp_at, 2**level), 2)
        place = pl.ds(pl.multiple_of(side * rank, rank), rank)
        stacks[level, place, :] = basis
        copy = pltpu.make_async_remote_copy(
            src_ref=stacks.at[level, place, :],
            dst_ref=stacks.at[level, place, :],
            send_sem=lsend.at[level],
            recv_sem=lrecv.at[level],
            device_id=(front_at, flip(grp_at, 2**level)),
            device_id_type=MESH,
        )
        copy.start()
        return copy

    def begin_solve(at):
        basis = bases[at]
        gram = lax.dot_general(
            basis, basis, (((1,), (1,)), ((), ())), precision=HIGHEST, preferred_element_type=jnp.float32
        )
        shift = 0.1 * (jnp.sum(gram * ident, keepdims=True) / rank) + 1e-05
        gram = gram + shift * ident
        scale = 1.0 / jnp.sum(gram * ident, keepdims=True)
        grams[at] = gram
        rest = ident - gram * scale
        state[at, pl.ds(0, rank), :] = (ident + rest) * scale
        state[at, pl.ds(rank, rank), :] = split_dot(rest, rest)

    def advance(systems, count):
        def step(_, carry):
            for at in systems:
                now = state[at]
                grown = split_dot(now, now[rank:])
                state[at, pl.ds(0, rank), :] = now[:rank] + grown[:rank]
                state[at, pl.ds(rank, rank), :] = grown[rank:]
            return carry

        lax.fori_loop(0, count, step, 0)

    def refine(systems):
        approx = {at: state[at, pl.ds(0, rank), :] for at in systems}
        for _ in range(EXACT_STEPS):
            inner = {at: 2.0 * ident - full_dot(grams[at], approx[at]) for at in systems}
            approx = {at: full_dot(approx[at], inner[at]) for at in systems}
        return approx

    def lift(systems, approx):
        return {at: full_dot(jnp.transpose(bases[at]), approx[at]) for at in systems}

    def put(source, target, at):
        copy = pltpu.make_async_copy(source, target, out_sem.at[at])
        copy.start()
        return copy

    def write_leaf(lifted):
        small = halves(jnp.dot(landed, jnp.concatenate(split(lifted), axis=1), preferred_element_type=jnp.float32))
        small = jnp.concatenate(split(small), axis=1)
        spot = lax.broadcasted_iota(jnp.int32, (leaf_ref.shape[0], devices * kept), 0).astype(jnp.float32)
        leaf_ref[...] = halves(jnp.dot(as_bf16(spot == where_to), small, preferred_element_type=jnp.float32))
        outputs.append(put(leaf_ref, leaf_hbm, LEVELS))

    def write_nodes(levels, lifted):
        for level in levels:
            node_ref[level] = split_dot(stacks[level], lifted[level + 1])
        for level in levels:
            outputs.append(put(node_ref.at[level], node_hbm.at[level], level))

    def end_sends():
        for copy in given + list(arrivals.values()) + [final]:
            copy.wait_send()

        def deliver_end(step, carry):
            deliver(step).wait_send()
            return carry

        lax.fori_loop(1, devices, deliver_end, 0)

    outputs = []
    total = STEPS - EXACT_STEPS - 1
    early = total // 2
    late = total - early
    copies = [offer(0, jnp.dot(chosen, landed, preferred_element_type=jnp.float32))]
    begin_solve(0)
    advance([0], early)
    end_sends()
    for level in range(LEVELS):
        copies[level].wait_recv()
        basis = take_rows(picks[level], stacks[level])
        if level < LEVELS - 1:
            copies.append(offer(level + 1, basis))
        else:
            bases[LEVELS] = basis
            outputs.append(put(bases.at[LEVELS], top_hbm, LEVELS + 1))
        begin_solve(level + 1)
        if level == 0:
            advance([0, 1], late)
        elif level == 1:
            advance([1, 2], early)
            write_leaf(lift([0], refine([0]))[0])
        else:
            advance([2, 3], late)
    now = state[LEVELS]
    lower = list(range(1, LEVELS))
    for number in range(early):
        if number == 1:
            approx = refine(lower)
        if number == 4:
            lifted = lift(lower, approx)
        if number == 6:
            write_nodes(range(LEVELS - 1), lifted)
        grown = split_dot(now, now[rank:])
        now = jnp.concatenate([now[:rank] + grown[:rank], grown[rank:]], axis=0)
    state[LEVELS] = now
    write_nodes([LEVELS - 1], lift([LEVELS], refine([LEVELS])))
    for copy in copies:
        copy.wait_send()
    for copy in outputs:
        copy.wait()


def local(
    contributions,
    sketch_matrix,
    destinations,
    parent_rows,
    front_sizes,
    leaf_skeleton,
    merge_skeleton,
):
    fronts, leaves = lax.axis_size("front"), lax.axis_size("grp")
    devices = fronts * leaves
    rows, order = contributions.shape
    depth, width = sketch_matrix.shape
    rank = leaf_skeleton.shape[-1]
    count = devices // 2
    capacity = 2 * rows // devices
    lines = -(-capacity * (width // 128) // 16) * 16
    hbm = pl.BlockSpec(memory_space=pl.ANY)
    semaphores = [
        (fronts // 2 + 1,), (5,), (LEVELS + 2,), (fronts // 2,), (fronts // 2,), (CUTS, count), (CUTS, count), (2,),
        (devices,), (devices,), (LEVELS,), (LEVELS,),
    ]
    leaf_map, node_maps, top_rows = pl.pallas_call(
        functools.partial(whole_kernel, fronts, leaves, capacity),
        out_shape=(
            jax.ShapeDtypeStruct((PR_DEV, rank), jnp.float32),
            jax.ShapeDtypeStruct((LEVELS, 2 * rank, rank), jnp.float32),
            jax.ShapeDtypeStruct((rank, width), jnp.float32),
        ),
        in_specs=[hbm] * 7,
        out_specs=(hbm, hbm, hbm),
        scratch_shapes=[
            pltpu.VMEM((devices, rows), jnp.int32),
            pltpu.VMEM((devices, rows), jnp.int32),
            pltpu.VMEM((1, rows), jnp.int32),
            pltpu.VMEM((1, rank), jnp.int32),
            pltpu.VMEM((merge_skeleton.shape[1], 1, rank), jnp.int32),
            pltpu.VMEM((PR_DEV, rank), jnp.float32),
            pltpu.VMEM((LEVELS, 2 * rank, rank), jnp.float32),
            pltpu.VMEM((2, rows, order // 2), jnp.bfloat16),
            pltpu.VMEM((count, depth, width), jnp.bfloat16),
            pltpu.VMEM((2 * rows, width), jnp.float32),
            pltpu.VMEM((rows, width), jnp.float32),
            pltpu.VMEM((devices, lines, 128), jnp.bfloat16),
            pltpu.VMEM((devices, lines, 128), jnp.bfloat16),
            pltpu.VMEM((LEVELS, 2 * rank, width), jnp.float32),
            pltpu.VMEM((LEVELS + 1, rank, width), jnp.float32),
            pltpu.VMEM((LEVELS + 1, rank, rank), jnp.float32),
            pltpu.VMEM((LEVELS + 1, 2 * rank, rank), jnp.float32),
        ]
        + [pltpu.SemaphoreType.DMA(shape) for shape in semaphores],
        compiler_params=pltpu.CompilerParams(
            collective_id=0, has_side_effects=True, vmem_limit_bytes=62 * 2**20
        ),
        cost_estimate=pl.CostEstimate(
            flops=2 * rows * order * width, bytes_accessed=2 * rows * order, transcendentals=0
        ),
    )(
        contributions,
        sketch_matrix,
        destinations.reshape(devices, rows),
        parent_rows.reshape(devices, rows),
        jnp.broadcast_to(front_sizes[None, :], (1, rows)),
        leaf_skeleton[0],
        merge_skeleton.reshape(merge_skeleton.shape[1], 1, rank),
    )
    return (leaf_map[None], node_maps[None, None], top_rows[None, None])


def solution(mesh):
    in_specs = (
        P(("front", "grp"), None),
        P(("front", "grp"), None),
        P(),
        P(),
        P("front"),
        P("front", "grp", None),
        P("front", None, None),
    )
    out_specs = (
        P("front", "grp", None),
        P("front", "grp", None, None, None),
        P("front", "grp", None, None),
    )
    return jax.shard_map(local, mesh=mesh, in_specs=in_specs, out_specs=out_specs, check_vma=False)
```

```python
import functools
import heapq

import jax
import jax.numpy as jnp
from jax import lax
from jax.experimental import pallas as pl
from jax.experimental.pallas import tpu as pltpu
from jax.sharding import PartitionSpec as P

PR_DEV = 1024
LEVELS = 3
STEPS = 24
EXACT_STEPS = 1
CUTS = 4
SHARES = 4
HIGHEST = lax.Precision.HIGHEST
MESH = pl.DeviceIdType.MESH


def bits_of(count):
    return count.bit_length() - 1


def flip(value, mask):
    bit = 1
    while bit <= mask:
        if mask & bit:
            value = value + bit * (1 - 2 * lax.rem(lax.div(value, bit), 2))
        bit *= 2
    return value


def exchange_plan(grp_bits, x_bits, cuts):
    grp = [1 << b for b in reversed(range(grp_bits))]
    xs = [1 << (grp_bits + b) for b in reversed(range(x_bits))]
    half = grp_bits // 2
    near = grp[-half:]
    orders = (grp[:1] + xs + grp[1:], grp[:1] + near + grp[1 : len(grp) - half] + xs)
    link = {d: "x" if d in xs else "near" if d in near else "far" for d in grp + xs}
    free = {}
    events = [(0.0, part, 0) for part in range(cuts)]
    sequence = []
    while events:
        now, part, slot = heapq.heappop(events)
        order = orders[part % 2]
        last = max([order.index(d) for d in order if d & slot], default=-1)
        onward = order[last + 1 :]
        sequence.append((part, slot, onward))
        for dim in onward:
            begin = max(now, free.get(link[dim], 0.0))
            free[link[dim]] = begin + 1.0
            heapq.heappush(events, (begin + 1.0 + 0.2 * cuts, part, slot ^ dim))
    return sequence


def split(value):
    high = value.astype(jnp.bfloat16)
    return high, (value - high.astype(jnp.float32)).astype(jnp.bfloat16)


def halves(value):
    width = value.shape[1] // 2
    return value[:, :width] + value[:, width:]


def split_dot(left, right):
    lh, ll = split(left)
    rh, rl = split(right)
    both = jnp.concatenate([lh, ll], axis=1)
    top = jnp.concatenate([rh, rl], axis=1)
    low = jnp.concatenate([rh, jnp.zeros_like(rl)], axis=1)
    weights = jnp.concatenate([top, low], axis=0)
    return halves(jnp.dot(both, weights, preferred_element_type=jnp.float32))


def full_dot(left, right):
    return jnp.dot(left, right, precision=HIGHEST, preferred_element_type=jnp.float32)


def take_rows(picker, rows):
    width = rows.shape[1]
    high, rest = split(rows)
    rest = rows - high.astype(jnp.float32)
    middle, low = split(rest)
    parts = jnp.concatenate([high, middle, low], axis=1)
    found = jnp.dot(picker, parts, preferred_element_type=jnp.float32)
    return (found[:, :width] + found[:, width : 2 * width]) + found[:, 2 * width :]


def as_bf16(condition):
    return condition.astype(jnp.float32).astype(jnp.bfloat16)


def column_of(line):
    return jnp.transpose(jnp.broadcast_to(line.astype(jnp.float32), (128, line.shape[1])))


def whole_kernel(
    fronts, leaves, capacity,
    c_ref, omega_ref, dest_hbm, prow_hbm, size_hbm, leafskel_hbm, mergeskel_hbm,
    leaf_hbm, node_hbm, top_hbm,
    dest_ref, prow_ref, size_ref, leafskel_ref, mergeskel_ref, leaf_ref, node_ref,
    cols, slots, acc, partial, packed, arrived, stacks, bases, grams, state,
    local_sem, table_sem, out_sem, csend, crecv, send, recv, psem, asend, arecv, lsend, lrecv,
):
    front_at = lax.axis_index("front")
    grp_at = lax.axis_index("grp")
    core = lax.rem(front_at, 2)
    x_at = lax.div(front_at, 2)
    devices = fronts * leaves
    myself = front_at * leaves + grp_at
    x_count = fronts // 2
    grp_bits, x_bits = bits_of(leaves), bits_of(x_count)
    depth = omega_ref.shape[0]
    cut = depth // CUTS
    rows, width = c_ref.shape[0], omega_ref.shape[1]
    span = leaves * depth
    rank = leafskel_ref.shape[1]
    sibling = (x_at * 2 + 1 - core, grp_at)

    def device(number):
        return (lax.div(number, leaves), lax.rem(number, leaves))

    def partner(dim):
        if dim < leaves:
            return (front_at, flip(grp_at, dim))
        return (flip(x_at, dim // leaves) * 2 + core, grp_at)

    tables = [
        (dest_hbm, dest_ref), (prow_hbm, prow_ref), (size_hbm, size_ref),
        (leafskel_hbm, leafskel_ref), (mergeskel_hbm, mergeskel_ref),
    ]
    tables = [pltpu.make_async_copy(a, b, table_sem.at[at]) for at, (a, b) in enumerate(tables)]
    barrier = pltpu.get_barrier_semaphore()

    def greet(step, carry):
        other = device(lax.rem(myself + step, devices))
        pl.semaphore_signal(barrier, inc=1, device_id=other, device_id_type=MESH)
        return carry

    lax.fori_loop(1, devices, greet, 0)
    mine = []
    for x in range(x_count):
        begin = pl.multiple_of((x * 2 + core) * span, 128)
        copy = pltpu.make_async_copy(
            c_ref.at[:, pl.ds(begin, span)], cols.at[0, :, pl.ds(x * span, span)], local_sem.at[x]
        )
        copy.start()
        mine.append(copy)
    copy = pltpu.make_async_copy(omega_ref, slots.at[0], local_sem.at[x_count])
    copy.start()
    mine.append(copy)
    for copy in tables:
        copy.start()
    pl.semaphore_wait(barrier, devices - 1)

    def start(part, slot, dim):
        source = omega_ref if slot == 0 else slots.at[slot]
        copy = pltpu.make_async_remote_copy(
            src_ref=source.at[pl.ds(part * cut, cut), :],
            dst_ref=slots.at[slot ^ dim, pl.ds(part * cut, cut), :],
            send_sem=send.at[part, slot ^ dim],
            recv_sem=recv.at[part, slot ^ dim],
            device_id=partner(dim),
            device_id_type=MESH,
        )
        copy.start()
        return copy

    sequence = exchange_plan(grp_bits, x_bits, CUTS)
    arrivals = {}
    given = []
    for part, slot, onward in sequence:
        if slot == 0:
            for dim in onward:
                arrivals[part, dim] = start(part, slot, dim)
    for x in range(x_count):
        begin = pl.multiple_of((x * 2 + 1 - core) * span, 128)
        copy = pltpu.make_async_remote_copy(
            src_ref=c_ref.at[:, pl.ds(begin, span)],
            dst_ref=cols.at[1, :, pl.ds(x * span, span)],
            send_sem=csend.at[x],
            recv_sem=crecv.at[x],
            device_id=sibling,
            device_id_type=MESH,
        )
        copy.start()
        given.append(copy)

    acc[...] = jnp.zeros_like(acc)

    chunks = width // 128
    used = capacity * chunks
    lines = packed.shape[1]
    kept = capacity if capacity % 8 == 0 else lines

    def make_tables():
        for copy in tables:
            copy.wait()
        shape = (devices, lines, rows)
        block_at = lax.broadcasted_iota(jnp.int32, shape, 0).astype(jnp.float32)
        line_at = lax.broadcasted_iota(jnp.int32, shape, 1)
        slot_at = jnp.where(line_at < used, lax.rem(line_at, capacity), -1).astype(jnp.float32)
        row = lax.broadcasted_iota(jnp.int32, (rows, rows), 0)
        col = lax.broadcasted_iota(jnp.int32, (rows, rows), 1)
        going = dest_ref[pl.ds(myself, 1), :].astype(jnp.float32)
        same = (column_of(going)[:, :rows] == going) & (row < col)
        rank_in = jnp.sum(same.astype(jnp.float32), axis=0, keepdims=True)
        placing = as_bf16((block_at == going.reshape(1, 1, rows)) & (slot_at == rank_in.reshape(1, 1, rows)))
        placing = placing.reshape(devices * lines, rows)

        coming = dest_ref[...] == myself
        ahead = jnp.dot(as_bf16(coming), as_bf16(row < col), preferred_element_type=jnp.float32)
        ahead = jnp.where(coming, ahead, -2.0)
        live = prow_ref[...] + grp_at * PR_DEV < size_ref[0]
        landing = jnp.where(live, prow_ref[...] + 1, 0).astype(jnp.float32)
        hit = ahead.reshape(devices, 1, rows) == slot_at[:, :kept, :]
        where_to = jnp.sum(jnp.where(hit, landing.reshape(devices, 1, rows), 0.0), axis=2, keepdims=True) - 1.0
        where_to = where_to.reshape(devices * kept, 1)
        where_to = jnp.transpose(jnp.broadcast_to(where_to, (devices * kept, 128)))[0:1, :]
        chosen = as_bf16(column_of(leafskel_ref[...])[:, 0:1] == where_to)
        picks = []
        for level in range(LEVELS):
            node = leaves - leaves // 2**level + lax.div(grp_at, 2 ** (level + 1))
            wanted = column_of(mergeskel_ref[node])[:, 0:1]
            at = lax.broadcasted_iota(jnp.int32, (rank, 2 * rank), 1).astype(jnp.float32)
            picks.append(as_bf16(wanted == at))
        return placing, where_to, chosen, picks

    def multiply(slot):
        x_from = flip(x_at, slot // leaves)
        grp_from = flip(grp_at, slot % leaves)
        begin = pl.multiple_of((x_from * leaves + grp_from) * depth, 128)
        left = cols[:, :, pl.ds(begin, depth)].reshape(2 * rows, depth)
        acc[...] += jnp.dot(left, slots[slot], preferred_element_type=jnp.float32)

    held = {}
    forwards = max(at for at, item in enumerate(sequence) if item[2])
    ready = False
    waiting = []
    for number, (part, slot, onward) in enumerate(sequence):
        if slot != 0:
            arrivals[part, slot].wait_recv()
            for dim in onward:
                arrivals[part, slot ^ dim] = start(part, slot, dim)
        held[slot] = held.get(slot, 0) + 1
        if held[slot] == CUTS:
            waiting.append(slot)
        if number >= len(sequence) // 4:
            if not ready:
                for copy in mine:
                    copy.wait()
                for copy in given:
                    copy.wait_recv()
                ready = True
            if waiting:
                multiply(waiting.pop(0))
        if number == forwards:
            placing, where_to, chosen, picks = make_tables()
    for item in waiting:
        multiply(item)

    final = pltpu.make_async_remote_copy(
        src_ref=acc.at[pl.ds(rows, rows), :],
        dst_ref=partial,
        send_sem=psem.at[0],
        recv_sem=psem.at[1],
        device_id=sibling,
        device_id_type=MESH,
    )
    final.start()
    final.wait_recv()
    sketch = (acc[pl.ds(0, rows), :] + partial[...]).astype(jnp.bfloat16)

    placed = jnp.dot(placing, sketch, preferred_element_type=jnp.float32).reshape(devices, lines, width)
    line = lax.broadcasted_iota(jnp.int32, (devices, lines, 128), 1)
    chunk_at = lax.div(line, capacity)
    sent = placed[:, :, :128]
    for chunk in range(1, chunks):
        sent = jnp.where(chunk_at == chunk, placed[:, :, chunk * 128 : (chunk + 1) * 128], sent)
    packed[...] = sent.astype(jnp.bfloat16)

    def deliver(step):
        number = lax.rem(myself + step, devices)
        return pltpu.make_async_remote_copy(
            src_ref=packed.at[number],
            dst_ref=arrived.at[myself],
            send_sem=asend.at[step],
            recv_sem=arecv.at[step],
            device_id=device(number),
            device_id_type=MESH,
        )

    def deliver_start(step, carry):
        deliver(step).start()
        return carry

    lax.fori_loop(1, devices, deliver_start, 0)
    arrived[pl.ds(myself, 1)] = packed[pl.ds(myself, 1)]

    def deliver_wait(step, carry):
        number = lax.rem(myself + devices - step, devices)
        pltpu.make_async_remote_copy(
            src_ref=packed.at[number],
            dst_ref=arrived.at[number],
            send_sem=asend.at[step],
            recv_sem=arecv.at[step],
            device_id=device(number),
            device_id_type=MESH,
        ).wait_recv()
        return carry

    lax.fori_loop(1, devices, deliver_wait, 0)
    flat = arrived[...].astype(jnp.float32)
    if kept == capacity:
        wide = [flat[:, chunk * capacity : (chunk + 1) * capacity] for chunk in range(chunks)]
    else:
        wide = [jnp.where(chunk_at == chunk, flat, 0.0) for chunk in range(chunks)]
    landed = jnp.concatenate(wide, axis=2).reshape(devices * kept, width).astype(jnp.bfloat16)

    eye_row = lax.broadcasted_iota(jnp.int32, (rank, rank), 0)
    ident = (eye_row == lax.broadcasted_iota(jnp.int32, (rank, rank), 1)).astype(jnp.float32)

    def offer(level, basis):
        bases[level] = basis
        side = lax.rem(lax.div(grp_at, 2**level), 2)
        place = pl.ds(pl.multiple_of(side * rank, rank), rank)
        stacks[level, place, :] = basis
        copy = pltpu.make_async_remote_copy(
            src_ref=stacks.at[level, place, :],
            dst_ref=stacks.at[level, place, :],
            send_sem=lsend.at[level],
            recv_sem=lrecv.at[level],
            device_id=(front_at, flip(grp_at, 2**level)),
            device_id_type=MESH,
        )
        copy.start()
        return copy

    def begin_solve(at):
        basis = bases[at]
        gram = lax.dot_general(
            basis, basis, (((1,), (1,)), ((), ())), precision=HIGHEST, preferred_element_type=jnp.float32
        )
        shift = 0.1 * (jnp.sum(gram * ident, keepdims=True) / rank) + 1e-05
        gram = gram + shift * ident
        scale = 1.0 / jnp.sum(gram * ident, keepdims=True)
        grams[at] = gram
        rest = ident - gram * scale
        state[at, pl.ds(0, rank), :] = (ident + rest) * scale
        state[at, pl.ds(rank, rank), :] = split_dot(rest, rest)

    def advance(systems, count):
        def step(_, carry):
            for at in systems:
                now = state[at]
                grown = split_dot(now, now[rank:])
                state[at, pl.ds(0, rank), :] = now[:rank] + grown[:rank]
                state[at, pl.ds(rank, rank), :] = grown[rank:]
            return carry

        lax.fori_loop(0, count, step, 0)

    def refine(systems):
        approx = {at: state[at, pl.ds(0, rank), :] for at in systems}
        for _ in range(EXACT_STEPS):
            inner = {at: 2.0 * ident - full_dot(grams[at], approx[at]) for at in systems}
            approx = {at: full_dot(approx[at], inner[at]) for at in systems}
        return approx

    def lift(systems, approx):
        return {at: full_dot(jnp.transpose(bases[at]), approx[at]) for at in systems}

    def put(source, target, at):
        copy = pltpu.make_async_copy(source, target, out_sem.at[at])
        copy.start()
        return copy

    def write_leaf(lifted):
        small = halves(jnp.dot(landed, jnp.concatenate(split(lifted), axis=1), preferred_element_type=jnp.float32))
        small = jnp.concatenate(split(small), axis=1)
        spot = lax.broadcasted_iota(jnp.int32, (leaf_ref.shape[0], devices * kept), 0).astype(jnp.float32)
        leaf_ref[...] = halves(jnp.dot(as_bf16(spot == where_to), small, preferred_element_type=jnp.float32))
        outputs.append(put(leaf_ref, leaf_hbm, LEVELS))

    def write_nodes(levels, lifted):
        for level in levels:
            node_ref[level] = split_dot(stacks[level], lifted[level + 1])
        for level in levels:
            outputs.append(put(node_ref.at[level], node_hbm.at[level], level))

    def end_sends():
        for copy in given + list(arrivals.values()) + [final]:
            copy.wait_send()

        def deliver_end(step, carry):
            deliver(step).wait_send()
            return carry

        lax.fori_loop(1, devices, deliver_end, 0)

    outputs = []
    total = STEPS - EXACT_STEPS - 1
    early = total // 2
    late = total - early
    ahead = 5
    copies = [offer(0, jnp.dot(chosen, landed, preferred_element_type=jnp.float32))]
    begin_solve(0)
    advance([0], early)
    end_sends()
    for level in range(LEVELS):
        copies[level].wait_recv()
        basis = take_rows(picks[level], stacks[level])
        if level < LEVELS - 1:
            copies.append(offer(level + 1, basis))
        else:
            bases[LEVELS] = basis
            outputs.append(put(bases.at[LEVELS], top_hbm, LEVELS + 1))
        begin_solve(level + 1)
        if level == 0:
            advance([0, 1], late)
        elif level == 1:
            advance([1, 2], early)
            advance([2], ahead)
            write_leaf(lift([0], refine([0]))[0])
        else:
            advance([2, 3], late - ahead)
    now = state[LEVELS]
    lower = list(range(1, LEVELS))
    for number in range(early + ahead):
        if number == 1:
            approx = refine(lower)
        if number == 4:
            lifted = lift(lower, approx)
        if number == 6:
            write_nodes(range(LEVELS - 1), lifted)
        grown = split_dot(now, now[rank:])
        now = jnp.concatenate([now[:rank] + grown[:rank], grown[rank:]], axis=0)
    state[LEVELS] = now
    write_nodes([LEVELS - 1], lift([LEVELS], refine([LEVELS])))
    for copy in copies:
        copy.wait_send()
    for copy in outputs:
        copy.wait()


def hand_on(*refs):
    sources, targets, sem = refs[:3], refs[3:6], refs[6]
    copies = []
    for at, (source, target) in enumerate(zip(sources, targets)):
        share = source.shape[-2] // SHARES
        for part in range(SHARES):
            place = (slice(None),) * (len(source.shape) - 2) + (pl.ds(part * share, share),)
            copies.append(pltpu.make_async_copy(source.at[place], target.at[place], sem.at[at, part]))
    for copy in copies:
        copy.start()
    for copy in copies:
        copy.wait()


def local(
    contributions,
    sketch_matrix,
    destinations,
    parent_rows,
    front_sizes,
    leaf_skeleton,
    merge_skeleton,
):
    fronts, leaves = lax.axis_size("front"), lax.axis_size("grp")
    devices = fronts * leaves
    rows, order = contributions.shape
    depth, width = sketch_matrix.shape
    rank = leaf_skeleton.shape[-1]
    count = devices // 2
    capacity = 2 * rows // devices
    lines = -(-capacity * (width // 128) // 16) * 16
    hbm = pl.BlockSpec(memory_space=pl.ANY)
    semaphores = [
        (fronts // 2 + 1,), (5,), (LEVELS + 2,), (fronts // 2,), (fronts // 2,), (CUTS, count), (CUTS, count), (2,),
        (devices,), (devices,), (LEVELS,), (LEVELS,),
    ]
    results = pl.pallas_call(
        functools.partial(whole_kernel, fronts, leaves, capacity),
        out_shape=(
            jax.ShapeDtypeStruct((PR_DEV, rank), jnp.float32),
            jax.ShapeDtypeStruct((LEVELS, 2 * rank, rank), jnp.float32),
            jax.ShapeDtypeStruct((rank, width), jnp.float32),
        ),
        in_specs=[hbm] * 7,
        out_specs=(hbm, hbm, hbm),
        scratch_shapes=[
            pltpu.VMEM((devices, rows), jnp.int32),
            pltpu.VMEM((devices, rows), jnp.int32),
            pltpu.SMEM((1,), jnp.int32),
            pltpu.VMEM((1, rank), jnp.int32),
            pltpu.VMEM((merge_skeleton.shape[1], 1, rank), jnp.int32),
            pltpu.VMEM((PR_DEV, rank), jnp.float32),
            pltpu.VMEM((LEVELS, 2 * rank, rank), jnp.float32),
            pltpu.VMEM((2, rows, order // 2), jnp.bfloat16),
            pltpu.VMEM((count, depth, width), jnp.bfloat16),
            pltpu.VMEM((2 * rows, width), jnp.float32),
            pltpu.VMEM((rows, width), jnp.float32),
            pltpu.VMEM((devices, lines, 128), jnp.bfloat16),
            pltpu.VMEM((devices, lines, 128), jnp.bfloat16),
            pltpu.VMEM((LEVELS, 2 * rank, width), jnp.float32),
            pltpu.VMEM((LEVELS + 1, rank, width), jnp.float32),
            pltpu.VMEM((LEVELS + 1, rank, rank), jnp.float32),
            pltpu.VMEM((LEVELS + 1, 2 * rank, rank), jnp.float32),
        ]
        + [pltpu.SemaphoreType.DMA(shape) for shape in semaphores],
        compiler_params=pltpu.CompilerParams(
            collective_id=0, has_side_effects=True, vmem_limit_bytes=62 * 2**20
        ),
        cost_estimate=pl.CostEstimate(
            flops=2 * rows * order * width, bytes_accessed=2 * rows * order, transcendentals=0
        ),
    )(
        contributions,
        sketch_matrix,
        destinations.reshape(devices, rows),
        parent_rows.reshape(devices, rows),
        front_sizes,
        leaf_skeleton[0],
        merge_skeleton.reshape(merge_skeleton.shape[1], 1, rank),
    )
    leaf_map, node_maps, top_rows = pl.pallas_call(
        hand_on,
        out_shape=[jax.ShapeDtypeStruct(result.shape, result.dtype) for result in results],
        in_specs=[hbm] * 3,
        out_specs=[hbm] * 3,
        scratch_shapes=[pltpu.SemaphoreType.DMA((3, SHARES))],
        compiler_params=pltpu.CompilerParams(vmem_limit_bytes=62 * 2**20),
    )(*results)
    return (leaf_map[None], node_maps[None, None], top_rows[None, None])


def solution(mesh):
    in_specs = (
        P(("front", "grp"), None),
        P(("front", "grp"), None),
        P(),
        P(),
        P("front"),
        P("front", "grp", None),
        P("front", None, None),
    )
    out_specs = (
        P("front", "grp", None),
        P("front", "grp", None, None, None),
        P("front", "grp", None, None),
    )
    return jax.shard_map(local, mesh=mesh, in_specs=in_specs, out_specs=out_specs, check_vma=False)
```

```python
import functools
import heapq

import jax
import jax.numpy as jnp
from jax import lax
from jax.experimental import pallas as pl
from jax.experimental.pallas import tpu as pltpu
from jax.sharding import PartitionSpec as P

PR_DEV = 1024
LEVELS = 3
STEPS = 24
EXACT_STEPS = 1
CUTS = 4
SHARES = 4
HIGHEST = lax.Precision.HIGHEST
MESH = pl.DeviceIdType.MESH


def bits_of(count):
    return count.bit_length() - 1


def flip(value, mask):
    bit = 1
    while bit <= mask:
        if mask & bit:
            value = value + bit * (1 - 2 * lax.rem(lax.div(value, bit), 2))
        bit *= 2
    return value


def exchange_plan(grp_bits, x_bits, cuts):
    grp = [1 << b for b in reversed(range(grp_bits))]
    xs = [1 << (grp_bits + b) for b in reversed(range(x_bits))]
    half = grp_bits // 2
    near = grp[-half:]
    orders = (grp[:1] + xs + grp[1:], grp[:1] + near + grp[1 : len(grp) - half] + xs)
    link = {d: "x" if d in xs else "near" if d in near else "far" for d in grp + xs}
    free = {}
    events = [(0.0, part, 0) for part in range(cuts)]
    sequence = []
    while events:
        now, part, slot = heapq.heappop(events)
        order = orders[part % 2]
        last = max([order.index(d) for d in order if d & slot], default=-1)
        onward = order[last + 1 :]
        sequence.append((part, slot, onward))
        for dim in onward:
            begin = max(now, free.get(link[dim], 0.0))
            free[link[dim]] = begin + 1.0
            heapq.heappush(events, (begin + 1.0 + 0.2 * cuts, part, slot ^ dim))
    return sequence


def split(value):
    high = value.astype(jnp.bfloat16)
    return high, (value - high.astype(jnp.float32)).astype(jnp.bfloat16)


def halves(value):
    width = value.shape[1] // 2
    return value[:, :width] + value[:, width:]


def split_dot(left, right):
    lh, ll = split(left)
    rh, rl = split(right)
    both = jnp.concatenate([lh, ll], axis=1)
    top = jnp.concatenate([rh, rl], axis=1)
    low = jnp.concatenate([rh, jnp.zeros_like(rl)], axis=1)
    weights = jnp.concatenate([top, low], axis=0)
    return halves(jnp.dot(both, weights, preferred_element_type=jnp.float32))


def full_dot(left, right):
    return jnp.dot(left, right, precision=HIGHEST, preferred_element_type=jnp.float32)


def take_rows(picker, rows):
    width = rows.shape[1]
    high, rest = split(rows)
    rest = rows - high.astype(jnp.float32)
    middle, low = split(rest)
    parts = jnp.concatenate([high, middle, low], axis=1)
    found = jnp.dot(picker, parts, preferred_element_type=jnp.float32)
    return (found[:, :width] + found[:, width : 2 * width]) + found[:, 2 * width :]


def as_bf16(condition):
    return condition.astype(jnp.float32).astype(jnp.bfloat16)


def column_of(line):
    return jnp.transpose(jnp.broadcast_to(line.astype(jnp.float32), (128, line.shape[1])))


def whole_kernel(
    fronts, leaves, capacity,
    c_ref, omega_ref, dest_hbm, prow_hbm, size_hbm, leafskel_hbm, mergeskel_hbm,
    leaf_hbm, node_hbm, top_hbm,
    dest_ref, prow_ref, size_ref, leafskel_ref, mergeskel_ref, leaf_ref, node_ref,
    cols, slots, acc, partial, packed, arrived, stacks, bases, grams, state,
    local_sem, table_sem, out_sem, csend, crecv, send, recv, psem, asend, arecv, lsend, lrecv,
):
    front_at = lax.axis_index("front")
    grp_at = lax.axis_index("grp")
    core = lax.rem(front_at, 2)
    x_at = lax.div(front_at, 2)
    devices = fronts * leaves
    myself = front_at * leaves + grp_at
    x_count = fronts // 2
    grp_bits, x_bits = bits_of(leaves), bits_of(x_count)
    depth = omega_ref.shape[0]
    cut = depth // CUTS
    rows, width = c_ref.shape[0], omega_ref.shape[1]
    span = leaves * depth
    rank = leafskel_ref.shape[1]
    sibling = (x_at * 2 + 1 - core, grp_at)

    def device(number):
        return (lax.div(number, leaves), lax.rem(number, leaves))

    def partner(dim):
        if dim < leaves:
            return (front_at, flip(grp_at, dim))
        return (flip(x_at, dim // leaves) * 2 + core, grp_at)

    tables = [
        (dest_hbm, dest_ref), (prow_hbm, prow_ref), (size_hbm, size_ref),
        (leafskel_hbm, leafskel_ref), (mergeskel_hbm, mergeskel_ref),
    ]
    tables = [pltpu.make_async_copy(a, b, table_sem.at[at]) for at, (a, b) in enumerate(tables)]
    barrier = pltpu.get_barrier_semaphore()

    def greet(step, carry):
        other = device(lax.rem(myself + step, devices))
        pl.semaphore_signal(barrier, inc=1, device_id=other, device_id_type=MESH)
        return carry

    lax.fori_loop(1, devices, greet, 0)
    mine = []
    for x in range(x_count):
        begin = pl.multiple_of((x * 2 + core) * span, 128)
        copy = pltpu.make_async_copy(
            c_ref.at[:, pl.ds(begin, span)], cols.at[0, :, pl.ds(x * span, span)], local_sem.at[x]
        )
        copy.start()
        mine.append(copy)
    copy = pltpu.make_async_copy(omega_ref, slots.at[0], local_sem.at[x_count])
    copy.start()
    mine.append(copy)
    for copy in tables:
        copy.start()
    pl.semaphore_wait(barrier, devices - 1)

    def start(part, slot, dim):
        source = omega_ref if slot == 0 else slots.at[slot]
        copy = pltpu.make_async_remote_copy(
            src_ref=source.at[pl.ds(part * cut, cut), :],
            dst_ref=slots.at[slot ^ dim, pl.ds(part * cut, cut), :],
            send_sem=send.at[part, slot ^ dim],
            recv_sem=recv.at[part, slot ^ dim],
            device_id=partner(dim),
            device_id_type=MESH,
        )
        copy.start()
        return copy

    sequence = exchange_plan(grp_bits, x_bits, CUTS)
    arrivals = {}
    given = []
    for part, slot, onward in sequence:
        if slot == 0:
            for dim in onward:
                arrivals[part, dim] = start(part, slot, dim)
    for x in range(x_count):
        begin = pl.multiple_of((x * 2 + 1 - core) * span, 128)
        copy = pltpu.make_async_remote_copy(
            src_ref=c_ref.at[:, pl.ds(begin, span)],
            dst_ref=cols.at[1, :, pl.ds(x * span, span)],
            send_sem=csend.at[x],
            recv_sem=crecv.at[x],
            device_id=sibling,
            device_id_type=MESH,
        )
        copy.start()
        given.append(copy)

    acc[...] = jnp.zeros_like(acc)

    chunks = width // 128
    used = capacity * chunks
    lines = packed.shape[1]
    kept = capacity if capacity % 8 == 0 else lines

    def make_tables():
        for copy in tables:
            copy.wait()
        shape = (devices, lines, rows)
        block_at = lax.broadcasted_iota(jnp.int32, shape, 0).astype(jnp.float32)
        line_at = lax.broadcasted_iota(jnp.int32, shape, 1)
        slot_at = jnp.where(line_at < used, lax.rem(line_at, capacity), -1).astype(jnp.float32)
        row = lax.broadcasted_iota(jnp.int32, (rows, rows), 0)
        col = lax.broadcasted_iota(jnp.int32, (rows, rows), 1)
        going = dest_ref[pl.ds(myself, 1), :].astype(jnp.float32)
        same = (column_of(going)[:, :rows] == going) & (row < col)
        rank_in = jnp.sum(same.astype(jnp.float32), axis=0, keepdims=True)
        placing = as_bf16((block_at == going.reshape(1, 1, rows)) & (slot_at == rank_in.reshape(1, 1, rows)))
        placing = placing.reshape(devices * lines, rows)

        coming = dest_ref[...] == myself
        ahead = jnp.dot(as_bf16(coming), as_bf16(row < col), preferred_element_type=jnp.float32)
        ahead = jnp.where(coming, ahead, -2.0)
        live = prow_ref[...] + grp_at * PR_DEV < size_ref[0]
        landing = jnp.where(live, prow_ref[...] + 1, 0).astype(jnp.float32)
        hit = ahead.reshape(devices, 1, rows) == slot_at[:, :kept, :]
        where_to = jnp.sum(jnp.where(hit, landing.reshape(devices, 1, rows), 0.0), axis=2, keepdims=True) - 1.0
        where_to = where_to.reshape(devices * kept, 1)
        where_to = jnp.transpose(jnp.broadcast_to(where_to, (devices * kept, 128)))[0:1, :]
        chosen = as_bf16(column_of(leafskel_ref[...])[:, 0:1] == where_to)
        picks = []
        for level in range(LEVELS):
            node = leaves - leaves // 2**level + lax.div(grp_at, 2 ** (level + 1))
            wanted = column_of(mergeskel_ref[node])[:, 0:1]
            at = lax.broadcasted_iota(jnp.int32, (rank, 2 * rank), 1).astype(jnp.float32)
            picks.append(as_bf16(wanted == at))
        return placing, where_to, chosen, picks

    def multiply(slot):
        x_from = flip(x_at, slot // leaves)
        grp_from = flip(grp_at, slot % leaves)
        begin = pl.multiple_of((x_from * leaves + grp_from) * depth, 128)
        left = cols[:, :, pl.ds(begin, depth)].reshape(2 * rows, depth)
        acc[...] += jnp.dot(left, slots[slot], preferred_element_type=jnp.float32)

    held = {}
    forwards = max(at for at, item in enumerate(sequence) if item[2])
    ready = False
    waiting = []
    for number, (part, slot, onward) in enumerate(sequence):
        if slot != 0:
            arrivals[part, slot].wait_recv()
            for dim in onward:
                arrivals[part, slot ^ dim] = start(part, slot, dim)
        held[slot] = held.get(slot, 0) + 1
        if held[slot] == CUTS:
            waiting.append(slot)
        if number >= len(sequence) // 4:
            if not ready:
                for copy in mine:
                    copy.wait()
                for copy in given:
                    copy.wait_recv()
                ready = True
            if waiting:
                multiply(waiting.pop(0))
        if number == forwards:
            placing, where_to, chosen, picks = make_tables()
    for item in waiting:
        multiply(item)

    final = pltpu.make_async_remote_copy(
        src_ref=acc.at[pl.ds(rows, rows), :],
        dst_ref=partial,
        send_sem=psem.at[0],
        recv_sem=psem.at[1],
        device_id=sibling,
        device_id_type=MESH,
    )
    final.start()
    final.wait_recv()
    sketch = (acc[pl.ds(0, rows), :] + partial[...]).astype(jnp.bfloat16)

    placed = jnp.dot(placing, sketch, preferred_element_type=jnp.float32).reshape(devices, lines, width)
    line = lax.broadcasted_iota(jnp.int32, (devices, lines, 128), 1)
    chunk_at = lax.div(line, capacity)
    sent = placed[:, :, :128]
    for chunk in range(1, chunks):
        sent = jnp.where(chunk_at == chunk, placed[:, :, chunk * 128 : (chunk + 1) * 128], sent)
    packed[...] = sent.astype(jnp.bfloat16)

    def deliver(step):
        number = lax.rem(myself + step, devices)
        return pltpu.make_async_remote_copy(
            src_ref=packed.at[number],
            dst_ref=arrived.at[myself],
            send_sem=asend.at[step],
            recv_sem=arecv.at[step],
            device_id=device(number),
            device_id_type=MESH,
        )

    def deliver_start(step, carry):
        deliver(step).start()
        return carry

    lax.fori_loop(1, devices, deliver_start, 0)
    arrived[pl.ds(myself, 1)] = packed[pl.ds(myself, 1)]

    def deliver_end(step, carry):
        deliver(step).wait_send()
        return carry

    def deliver_wait(step, carry):
        number = lax.rem(myself + devices - step, devices)
        pltpu.make_async_remote_copy(
            src_ref=packed.at[number],
            dst_ref=arrived.at[number],
            send_sem=asend.at[step],
            recv_sem=arecv.at[step],
            device_id=device(number),
            device_id_type=MESH,
        ).wait_recv()
        return carry

    for copy in given + list(arrivals.values()) + [final]:
        copy.wait_send()
    lax.fori_loop(1, devices, deliver_wait, 0)
    flat = arrived[...].astype(jnp.float32)
    if kept == capacity:
        wide = [flat[:, chunk * capacity : (chunk + 1) * capacity] for chunk in range(chunks)]
    else:
        wide = [jnp.where(chunk_at == chunk, flat, 0.0) for chunk in range(chunks)]
    landed = jnp.concatenate(wide, axis=2).reshape(devices * kept, width).astype(jnp.bfloat16)

    eye_row = lax.broadcasted_iota(jnp.int32, (rank, rank), 0)
    ident = (eye_row == lax.broadcasted_iota(jnp.int32, (rank, rank), 1)).astype(jnp.float32)

    def offer(level, chunk, basis):
        side = lax.rem(lax.div(grp_at, 2**level), 2)
        place = pl.ds(pl.multiple_of(side * rank, rank), rank)
        columns = pl.ds(chunk * 128, 128)
        bases[level, :, columns] = basis
        stacks[level, place, columns] = basis
        copy = pltpu.make_async_remote_copy(
            src_ref=stacks.at[level, place, columns],
            dst_ref=stacks.at[level, place, columns],
            send_sem=lsend.at[level, chunk],
            recv_sem=lrecv.at[level, chunk],
            device_id=(front_at, flip(grp_at, 2**level)),
            device_id_type=MESH,
        )
        copy.start()
        copies[level, chunk] = copy

    def merge(level, chunk):
        copies[level, chunk].wait_recv()
        columns = pl.ds(chunk * 128, 128)
        basis = take_rows(picks[level], stacks[level, :, columns])
        if level < LEVELS - 1:
            offer(level + 1, chunk, basis)
        else:
            bases[LEVELS, :, columns] = basis

    def begin_solve(at):
        basis = bases[at]
        gram = lax.dot_general(
            basis, basis, (((1,), (1,)), ((), ())), precision=HIGHEST, preferred_element_type=jnp.float32
        )
        shift = 0.1 * (jnp.sum(gram * ident, keepdims=True) / rank) + 1e-05
        gram = gram + shift * ident
        scale = 1.0 / jnp.sum(gram * ident, keepdims=True)
        grams[at] = gram
        rest = ident - gram * scale
        state[at, pl.ds(0, rank), :] = (ident + rest) * scale
        state[at, pl.ds(rank, rank), :] = split_dot(rest, rest)

    def advance(systems, count):
        def step(_, carry):
            for at in systems:
                now = state[at]
                grown = split_dot(now, now[rank:])
                state[at, pl.ds(0, rank), :] = now[:rank] + grown[:rank]
                state[at, pl.ds(rank, rank), :] = grown[rank:]
            return carry

        lax.fori_loop(0, count, step, 0)

    def refine(systems):
        approx = {at: state[at, pl.ds(0, rank), :] for at in systems}
        for _ in range(EXACT_STEPS):
            inner = {at: 2.0 * ident - full_dot(grams[at], approx[at]) for at in systems}
            approx = {at: full_dot(approx[at], inner[at]) for at in systems}
        return approx

    def lift(systems, approx):
        return {at: full_dot(jnp.transpose(bases[at]), approx[at]) for at in systems}

    def put(source, target, at):
        copy = pltpu.make_async_copy(source, target, out_sem.at[at])
        copy.start()
        return copy

    def write_leaf(lifted):
        small = halves(jnp.dot(landed, jnp.concatenate(split(lifted), axis=1), preferred_element_type=jnp.float32))
        small = jnp.concatenate(split(small), axis=1)
        spot = lax.broadcasted_iota(jnp.int32, (leaf_ref.shape[0], devices * kept), 0).astype(jnp.float32)
        leaf_ref[...] = halves(jnp.dot(as_bf16(spot == where_to), small, preferred_element_type=jnp.float32))
        outputs.append(put(leaf_ref, leaf_hbm, LEVELS))

    def write_nodes(levels, lifted):
        for level in levels:
            node_ref[level] = split_dot(stacks[level], lifted[level + 1])
        for level in levels:
            outputs.append(put(node_ref.at[level], node_hbm.at[level], level))

    outputs = []
    copies = {}
    total = STEPS - EXACT_STEPS - 1
    first, second, third = total // 4, total // 7, total // 10
    leaf_basis = jnp.dot(chosen, landed, preferred_element_type=jnp.float32)
    for chunk in range(chunks):
        offer(0, chunk, leaf_basis[:, chunk * 128 : (chunk + 1) * 128])
    begin_solve(0)
    advance([0], first)
    for chunk in range(chunks):
        merge(0, chunk)
        if chunk == 0:
            advance([0], second)
    begin_solve(1)
    for chunk in range(chunks):
        merge(1, chunk)
        if chunk == 0:
            advance([0, 1], third)
    begin_solve(2)
    left = total - first - second - third
    advance([0, 1, 2], left)
    lax.fori_loop(1, devices, deliver_end, 0)
    for chunk in range(chunks):
        merge(2, chunk)
    outputs.append(put(bases.at[LEVELS], top_hbm, LEVELS + 1))
    begin_solve(3)
    more = total - third - left
    advance([1, 2, 3], more)
    rest = total - left - more
    advance([2, 3], rest)
    now = state[LEVELS]
    lower = list(range(LEVELS))
    for number in range(total - more - rest):
        if number == 1:
            approx = refine(lower)
        if number == 4:
            lifted = lift(lower, approx)
        if number == 6:
            write_leaf(lifted[0])
        if number == 8:
            write_nodes(range(LEVELS - 1), lifted)
        grown = split_dot(now, now[rank:])
        now = jnp.concatenate([now[:rank] + grown[:rank], grown[rank:]], axis=0)
    state[LEVELS] = now
    write_nodes([LEVELS - 1], lift([LEVELS], refine([LEVELS])))
    for copy in copies.values():
        copy.wait_send()
    for copy in outputs:
        copy.wait()


def hand_on(*refs):
    sources, targets, held, sem = refs[:3], refs[3:6], refs[6:9], refs[9]
    into, out = [], []
    for at, (source, middle, target) in enumerate(zip(sources, held, targets)):
        share = source.shape[-2] // SHARES
        for part in range(SHARES):
            place = (slice(None),) * (len(source.shape) - 2) + (pl.ds(part * share, share),)
            into.append(pltpu.make_async_copy(source.at[place], middle.at[place], sem.at[0, at, part]))
            out.append(pltpu.make_async_copy(middle.at[place], target.at[place], sem.at[1, at, part]))
    for copy in into:
        copy.start()
    for first, second in zip(into, out):
        first.wait()
        second.start()
    for copy in out:
        copy.wait()


def local(
    contributions,
    sketch_matrix,
    destinations,
    parent_rows,
    front_sizes,
    leaf_skeleton,
    merge_skeleton,
):
    fronts, leaves = lax.axis_size("front"), lax.axis_size("grp")
    devices = fronts * leaves
    rows, order = contributions.shape
    depth, width = sketch_matrix.shape
    rank = leaf_skeleton.shape[-1]
    count = devices // 2
    capacity = 2 * rows // devices
    lines = -(-capacity * (width // 128) // 16) * 16
    hbm = pl.BlockSpec(memory_space=pl.ANY)
    semaphores = [
        (fronts // 2 + 1,), (5,), (LEVELS + 2,), (fronts // 2,), (fronts // 2,), (CUTS, count), (CUTS, count), (2,),
        (devices,), (devices,), (LEVELS, width // 128), (LEVELS, width // 128),
    ]
    results = pl.pallas_call(
        functools.partial(whole_kernel, fronts, leaves, capacity),
        out_shape=(
            jax.ShapeDtypeStruct((PR_DEV, rank), jnp.float32),
            jax.ShapeDtypeStruct((LEVELS, 2 * rank, rank), jnp.float32),
            jax.ShapeDtypeStruct((rank, width), jnp.float32),
        ),
        in_specs=[hbm] * 7,
        out_specs=(hbm, hbm, hbm),
        scratch_shapes=[
            pltpu.VMEM((devices, rows), jnp.int32),
            pltpu.VMEM((devices, rows), jnp.int32),
            pltpu.SMEM((1,), jnp.int32),
            pltpu.VMEM((1, rank), jnp.int32),
            pltpu.VMEM((merge_skeleton.shape[1], 1, rank), jnp.int32),
            pltpu.VMEM((PR_DEV, rank), jnp.float32),
            pltpu.VMEM((LEVELS, 2 * rank, rank), jnp.float32),
            pltpu.VMEM((2, rows, order // 2), jnp.bfloat16),
            pltpu.VMEM((count, depth, width), jnp.bfloat16),
            pltpu.VMEM((2 * rows, width), jnp.float32),
            pltpu.VMEM((rows, width), jnp.float32),
            pltpu.VMEM((devices, lines, 128), jnp.bfloat16),
            pltpu.VMEM((devices, lines, 128), jnp.bfloat16),
            pltpu.VMEM((LEVELS, 2 * rank, width), jnp.float32),
            pltpu.VMEM((LEVELS + 1, rank, width), jnp.float32),
            pltpu.VMEM((LEVELS + 1, rank, rank), jnp.float32),
            pltpu.VMEM((LEVELS + 1, 2 * rank, rank), jnp.float32),
        ]
        + [pltpu.SemaphoreType.DMA(shape) for shape in semaphores],
        compiler_params=pltpu.CompilerParams(
            collective_id=0, has_side_effects=True, vmem_limit_bytes=62 * 2**20
        ),
        cost_estimate=pl.CostEstimate(
            flops=2 * rows * order * width, bytes_accessed=2 * rows * order, transcendentals=0
        ),
    )(
        contributions,
        sketch_matrix,
        destinations.reshape(devices, rows),
        parent_rows.reshape(devices, rows),
        front_sizes,
        leaf_skeleton[0],
        merge_skeleton.reshape(merge_skeleton.shape[1], 1, rank),
    )
    leaf_map, node_maps, top_rows = pl.pallas_call(
        hand_on,
        out_shape=[jax.ShapeDtypeStruct(result.shape, result.dtype) for result in results],
        in_specs=[hbm] * 3,
        out_specs=[hbm] * 3,
        scratch_shapes=[pltpu.VMEM(result.shape, result.dtype) for result in results]
        + [pltpu.SemaphoreType.DMA((2, 3, SHARES))],
        compiler_params=pltpu.CompilerParams(vmem_limit_bytes=62 * 2**20),
    )(*results)
    return (leaf_map[None], node_maps[None, None], top_rows[None, None])


def solution(mesh):
    in_specs = (
        P(("front", "grp"), None),
        P(("front", "grp"), None),
        P(),
        P(),
        P("front"),
        P("front", "grp", None),
        P("front", None, None),
    )
    out_specs = (
        P("front", "grp", None),
        P("front", "grp", None, None, None),
        P("front", "grp", None, None),
    )
    return jax.shard_map(local, mesh=mesh, in_specs=in_specs, out_specs=out_specs, check_vma=False)
```

```python
import functools
import heapq

import jax
import jax.numpy as jnp
from jax import lax
from jax.experimental import pallas as pl
from jax.experimental.pallas import tpu as pltpu
from jax.sharding import PartitionSpec as P

PR_DEV = 1024
LEVELS = 3
STEPS = 24
EXACT_STEPS = 1
CUTS = 4
SHARES = 4
HIGHEST = lax.Precision.HIGHEST
MESH = pl.DeviceIdType.MESH


def bits_of(count):
    return count.bit_length() - 1


def flip(value, mask):
    bit = 1
    while bit <= mask:
        if mask & bit:
            value = value + bit * (1 - 2 * lax.rem(lax.div(value, bit), 2))
        bit *= 2
    return value


def exchange_plan(grp_bits, x_bits, cuts):
    grp = [1 << b for b in reversed(range(grp_bits))]
    xs = [1 << (grp_bits + b) for b in reversed(range(x_bits))]
    half = grp_bits // 2
    near = grp[-half:]
    orders = (grp[:1] + xs + grp[1:], grp[:1] + near + grp[1 : len(grp) - half] + xs)
    link = {d: "x" if d in xs else "near" if d in near else "far" for d in grp + xs}
    free = {}
    events = []
    sequence = [(part, 0, orders[part % 2]) for part in range(cuts)]

    def send(now, part, slot, dim):
        begin = max(now, free.get(link[dim], 0.0))
        free[link[dim]] = begin + 1.0
        heapq.heappush(events, (begin + 1.0 + 0.2 * cuts, part, slot ^ dim))

    for place in range(grp_bits + x_bits):
        for part in range(cuts):
            send(0.0, part, 0, orders[part % 2][place])
    while events:
        now, part, slot = heapq.heappop(events)
        order = orders[part % 2]
        last = max([order.index(d) for d in order if d & slot], default=-1)
        onward = order[last + 1 :]
        sequence.append((part, slot, onward))
        for dim in onward:
            send(now, part, slot, dim)
    return sequence


def split(value):
    high = value.astype(jnp.bfloat16)
    return high, (value - high.astype(jnp.float32)).astype(jnp.bfloat16)


def halves(value):
    width = value.shape[1] // 2
    return value[:, :width] + value[:, width:]


def split_dot(left, right):
    lh, ll = split(left)
    rh, rl = split(right)
    both = jnp.concatenate([lh, ll], axis=1)
    top = jnp.concatenate([rh, rl], axis=1)
    low = jnp.concatenate([rh, jnp.zeros_like(rl)], axis=1)
    weights = jnp.concatenate([top, low], axis=0)
    return halves(jnp.dot(both, weights, preferred_element_type=jnp.float32))


def full_dot(left, right):
    return jnp.dot(left, right, precision=HIGHEST, preferred_element_type=jnp.float32)


def take_rows(picker, rows):
    width = rows.shape[1]
    high, rest = split(rows)
    rest = rows - high.astype(jnp.float32)
    middle, low = split(rest)
    parts = jnp.concatenate([high, middle, low], axis=1)
    found = jnp.dot(picker, parts, preferred_element_type=jnp.float32)
    return (found[:, :width] + found[:, width : 2 * width]) + found[:, 2 * width :]


def as_bf16(condition):
    return condition.astype(jnp.float32).astype(jnp.bfloat16)


def column_of(line):
    return jnp.transpose(jnp.broadcast_to(line.astype(jnp.float32), (128, line.shape[1])))


def whole_kernel(
    fronts, leaves, capacity,
    c_ref, omega_ref, dest_hbm, prow_hbm, size_hbm, leafskel_hbm, mergeskel_hbm,
    leaf_hbm, node_hbm, top_hbm,
    dest_ref, prow_ref, size_ref, leafskel_ref, mergeskel_ref, leaf_ref, node_ref,
    cols, slots, acc, partial, packed, arrived, stacks, bases, grams, state,
    local_sem, table_sem, out_sem, csend, crecv, send, recv, psem, asend, arecv, lsend, lrecv,
):
    front_at = lax.axis_index("front")
    grp_at = lax.axis_index("grp")
    core = lax.rem(front_at, 2)
    x_at = lax.div(front_at, 2)
    devices = fronts * leaves
    myself = front_at * leaves + grp_at
    x_count = fronts // 2
    grp_bits, x_bits = bits_of(leaves), bits_of(x_count)
    depth = omega_ref.shape[0]
    cut = depth // CUTS
    rows, width = c_ref.shape[0], omega_ref.shape[1]
    span = leaves * depth
    rank = leafskel_ref.shape[1]
    sibling = (x_at * 2 + 1 - core, grp_at)

    def device(number):
        return (lax.div(number, leaves), lax.rem(number, leaves))

    def partner(dim):
        if dim < leaves:
            return (front_at, flip(grp_at, dim))
        return (flip(x_at, dim // leaves) * 2 + core, grp_at)

    tables = [
        (dest_hbm, dest_ref), (prow_hbm, prow_ref), (size_hbm, size_ref),
        (leafskel_hbm, leafskel_ref), (mergeskel_hbm, mergeskel_ref),
    ]
    tables = [pltpu.make_async_copy(a, b, table_sem.at[at]) for at, (a, b) in enumerate(tables)]
    barrier = pltpu.get_barrier_semaphore()

    def greet(step, carry):
        other = device(lax.rem(myself + step, devices))
        pl.semaphore_signal(barrier, inc=1, device_id=other, device_id_type=MESH)
        return carry

    lax.fori_loop(1, devices, greet, 0)
    mine = []
    for x in range(x_count):
        begin = pl.multiple_of((x * 2 + core) * span, 128)
        copy = pltpu.make_async_copy(
            c_ref.at[:, pl.ds(begin, span)], cols.at[0, :, pl.ds(x * span, span)], local_sem.at[x]
        )
        copy.start()
        mine.append(copy)
    copy = pltpu.make_async_copy(omega_ref, slots.at[0], local_sem.at[x_count])
    copy.start()
    mine.append(copy)
    for copy in tables:
        copy.start()
    pl.semaphore_wait(barrier, devices - 1)

    def start(part, slot, dim):
        source = omega_ref if slot == 0 else slots.at[slot]
        copy = pltpu.make_async_remote_copy(
            src_ref=source.at[pl.ds(part * cut, cut), :],
            dst_ref=slots.at[slot ^ dim, pl.ds(part * cut, cut), :],
            send_sem=send.at[part, slot ^ dim],
            recv_sem=recv.at[part, slot ^ dim],
            device_id=partner(dim),
            device_id_type=MESH,
        )
        copy.start()
        return copy

    sequence = exchange_plan(grp_bits, x_bits, CUTS)
    arrivals = {}
    given = []
    for place in range(grp_bits + x_bits):
        for part, slot, onward in sequence[:CUTS]:
            arrivals[part, onward[place]] = start(part, slot, onward[place])
    for x in range(x_count):
        begin = pl.multiple_of((x * 2 + 1 - core) * span, 128)
        copy = pltpu.make_async_remote_copy(
            src_ref=c_ref.at[:, pl.ds(begin, span)],
            dst_ref=cols.at[1, :, pl.ds(x * span, span)],
            send_sem=csend.at[x],
            recv_sem=crecv.at[x],
            device_id=sibling,
            device_id_type=MESH,
        )
        copy.start()
        given.append(copy)

    acc[...] = jnp.zeros_like(acc)

    chunks = width // 128
    used = capacity * chunks
    lines = packed.shape[1]
    kept = capacity if capacity % 8 == 0 else lines

    def make_tables():
        for copy in tables:
            copy.wait()
        shape = (devices, lines, rows)
        block_at = lax.broadcasted_iota(jnp.int32, shape, 0).astype(jnp.float32)
        line_at = lax.broadcasted_iota(jnp.int32, shape, 1)
        slot_at = jnp.where(line_at < used, lax.rem(line_at, capacity), -1).astype(jnp.float32)
        row = lax.broadcasted_iota(jnp.int32, (rows, rows), 0)
        col = lax.broadcasted_iota(jnp.int32, (rows, rows), 1)
        going = dest_ref[pl.ds(myself, 1), :].astype(jnp.float32)
        same = (column_of(going)[:, :rows] == going) & (row < col)
        rank_in = jnp.sum(same.astype(jnp.float32), axis=0, keepdims=True)
        placing = as_bf16((block_at == going.reshape(1, 1, rows)) & (slot_at == rank_in.reshape(1, 1, rows)))
        placing = placing.reshape(devices * lines, rows)

        coming = dest_ref[...] == myself
        ahead = jnp.dot(as_bf16(coming), as_bf16(row < col), preferred_element_type=jnp.float32)
        ahead = jnp.where(coming, ahead, -2.0)
        live = prow_ref[...] + grp_at * PR_DEV < size_ref[0]
        landing = jnp.where(live, prow_ref[...] + 1, 0).astype(jnp.float32)
        hit = ahead.reshape(devices, 1, rows) == slot_at[:, :kept, :]
        where_to = jnp.sum(jnp.where(hit, landing.reshape(devices, 1, rows), 0.0), axis=2, keepdims=True) - 1.0
        where_to = where_to.reshape(devices * kept, 1)
        where_to = jnp.transpose(jnp.broadcast_to(where_to, (devices * kept, 128)))[0:1, :]
        chosen = as_bf16(column_of(leafskel_ref[...])[:, 0:1] == where_to)
        picks = []
        for level in range(LEVELS):
            node = leaves - leaves // 2**level + lax.div(grp_at, 2 ** (level + 1))
            wanted = column_of(mergeskel_ref[node])[:, 0:1]
            at = lax.broadcasted_iota(jnp.int32, (rank, 2 * rank), 1).astype(jnp.float32)
            picks.append(as_bf16(wanted == at))
        return placing, where_to, chosen, picks

    def multiply(slot):
        x_from = flip(x_at, slot // leaves)
        grp_from = flip(grp_at, slot % leaves)
        begin = pl.multiple_of((x_from * leaves + grp_from) * depth, 128)
        left = cols[:, :, pl.ds(begin, depth)].reshape(2 * rows, depth)
        acc[...] += jnp.dot(left, slots[slot], preferred_element_type=jnp.float32)

    held = {}
    forwards = max(at for at, item in enumerate(sequence) if item[2])
    ready = False
    waiting = []
    for number, (part, slot, onward) in enumerate(sequence):
        if slot != 0:
            arrivals[part, slot].wait_recv()
            for dim in onward:
                arrivals[part, slot ^ dim] = start(part, slot, dim)
        held[slot] = held.get(slot, 0) + 1
        if held[slot] == CUTS:
            waiting.append(slot)
        if number >= len(sequence) // 4:
            if not ready:
                for copy in mine:
                    copy.wait()
                for copy in given:
                    copy.wait_recv()
                ready = True
            if waiting:
                multiply(waiting.pop(0))
        if number == forwards:
            placing, where_to, chosen, picks = make_tables()
    for item in waiting:
        multiply(item)

    final = pltpu.make_async_remote_copy(
        src_ref=acc.at[pl.ds(rows, rows), :],
        dst_ref=partial,
        send_sem=psem.at[0],
        recv_sem=psem.at[1],
        device_id=sibling,
        device_id_type=MESH,
    )
    final.start()
    final.wait_recv()
    sketch = (acc[pl.ds(0, rows), :] + partial[...]).astype(jnp.bfloat16)

    placed = jnp.dot(placing, sketch, preferred_element_type=jnp.float32).reshape(devices, lines, width)
    line = lax.broadcasted_iota(jnp.int32, (devices, lines, 128), 1)
    chunk_at = lax.div(line, capacity)
    sent = placed[:, :, :128]
    for chunk in range(1, chunks):
        sent = jnp.where(chunk_at == chunk, placed[:, :, chunk * 128 : (chunk + 1) * 128], sent)
    packed[...] = sent.astype(jnp.bfloat16)

    def deliver(step):
        number = lax.rem(myself + step, devices)
        return pltpu.make_async_remote_copy(
            src_ref=packed.at[number],
            dst_ref=arrived.at[myself],
            send_sem=asend.at[step],
            recv_sem=arecv.at[step],
            device_id=device(number),
            device_id_type=MESH,
        )

    for step in range(1, devices):
        deliver(step).start()
    arrived[pl.ds(myself, 1)] = packed[pl.ds(myself, 1)]

    def deliver_end(step, carry):
        deliver(step).wait_send()
        return carry

    def deliver_wait(step, carry):
        number = lax.rem(myself + devices - step, devices)
        pltpu.make_async_remote_copy(
            src_ref=packed.at[number],
            dst_ref=arrived.at[number],
            send_sem=asend.at[step],
            recv_sem=arecv.at[step],
            device_id=device(number),
            device_id_type=MESH,
        ).wait_recv()
        return carry

    for copy in given + list(arrivals.values()) + [final]:
        copy.wait_send()
    lax.fori_loop(1, devices, deliver_wait, 0)
    flat = arrived[...].astype(jnp.float32)
    if kept == capacity:
        wide = [flat[:, chunk * capacity : (chunk + 1) * capacity] for chunk in range(chunks)]
    else:
        wide = [jnp.where(chunk_at == chunk, flat, 0.0) for chunk in range(chunks)]
    landed = jnp.concatenate(wide, axis=2).reshape(devices * kept, width).astype(jnp.bfloat16)

    eye_row = lax.broadcasted_iota(jnp.int32, (rank, rank), 0)
    ident = (eye_row == lax.broadcasted_iota(jnp.int32, (rank, rank), 1)).astype(jnp.float32)

    def offer(level, chunk, basis):
        side = lax.rem(lax.div(grp_at, 2**level), 2)
        place = pl.ds(pl.multiple_of(side * rank, rank), rank)
        columns = pl.ds(chunk * 128, 128)
        bases[level, :, columns] = basis
        stacks[level, place, columns] = basis
        copy = pltpu.make_async_remote_copy(
            src_ref=stacks.at[level, place, columns],
            dst_ref=stacks.at[level, place, columns],
            send_sem=lsend.at[level, chunk],
            recv_sem=lrecv.at[level, chunk],
            device_id=(front_at, flip(grp_at, 2**level)),
            device_id_type=MESH,
        )
        copy.start()
        copies[level, chunk] = copy

    def merge(level, chunk):
        copies[level, chunk].wait_recv()
        columns = pl.ds(chunk * 128, 128)
        basis = take_rows(picks[level], stacks[level, :, columns])
        if level < LEVELS - 1:
            offer(level + 1, chunk, basis)
        else:
            bases[LEVELS, :, columns] = basis

    def begin_solve(at):
        basis = bases[at]
        gram = lax.dot_general(
            basis, basis, (((1,), (1,)), ((), ())), precision=HIGHEST, preferred_element_type=jnp.float32
        )
        trace = jnp.sum(gram * ident, keepdims=True)
        shift = 0.1 * (trace / rank) + 1e-05
        gram = gram + shift * ident
        scale = 1.0 / (trace + rank * shift)
        grams[at] = gram
        rest = ident - gram * scale
        state[at, pl.ds(0, rank), :] = (ident + rest) * scale
        state[at, pl.ds(rank, rank), :] = split_dot(rest, rest)

    def advance(systems, count):
        def step(_, carry):
            for at in systems:
                now = state[at]
                grown = split_dot(now, now[rank:])
                state[at, pl.ds(0, rank), :] = now[:rank] + grown[:rank]
                state[at, pl.ds(rank, rank), :] = grown[rank:]
            return carry

        lax.fori_loop(0, count, step, 0)

    def refine(systems):
        approx = {at: state[at, pl.ds(0, rank), :] for at in systems}
        for _ in range(EXACT_STEPS):
            inner = {at: 2.0 * ident - full_dot(grams[at], approx[at]) for at in systems}
            approx = {at: full_dot(approx[at], inner[at]) for at in systems}
        return approx

    def lift(systems, approx):
        return {at: full_dot(jnp.transpose(bases[at]), approx[at]) for at in systems}

    def put(source, target, at):
        copy = pltpu.make_async_copy(source, target, out_sem.at[at])
        copy.start()
        return copy

    def write_leaf(lifted):
        small = halves(jnp.dot(landed, jnp.concatenate(split(lifted), axis=1), preferred_element_type=jnp.float32))
        small = jnp.concatenate(split(small), axis=1)
        spot = lax.broadcasted_iota(jnp.int32, (leaf_ref.shape[0], devices * kept), 0).astype(jnp.float32)
        leaf_ref[...] = halves(jnp.dot(as_bf16(spot == where_to), small, preferred_element_type=jnp.float32))
        outputs.append(put(leaf_ref, leaf_hbm, LEVELS))

    def write_nodes(levels, lifted):
        for level in levels:
            node_ref[level] = split_dot(stacks[level], lifted[level + 1])
        for level in levels:
            outputs.append(put(node_ref.at[level], node_hbm.at[level], level))

    outputs = []
    copies = {}
    total = STEPS - EXACT_STEPS - 1
    first, second, third = total // 4, total // 7, total // 10
    leaf_basis = jnp.dot(chosen, landed, preferred_element_type=jnp.float32)
    for chunk in range(chunks):
        offer(0, chunk, leaf_basis[:, chunk * 128 : (chunk + 1) * 128])
    begin_solve(0)
    advance([0], first)
    for chunk in range(chunks):
        merge(0, chunk)
        if chunk == 0:
            advance([0], second)
    begin_solve(1)
    for chunk in range(chunks):
        merge(1, chunk)
        if chunk == 0:
            advance([0, 1], third)
    begin_solve(2)
    left = total - first - second - third
    advance([0, 1, 2], left)
    lax.fori_loop(1, devices, deliver_end, 0)
    for chunk in range(chunks):
        merge(2, chunk)
    outputs.append(put(bases.at[LEVELS], top_hbm, LEVELS + 1))
    begin_solve(3)
    more = total - third - left
    advance([1, 2, 3], more)
    rest = total - left - more
    advance([2, 3], rest)
    now = state[LEVELS]
    lower = list(range(LEVELS))
    for number in range(total - more - rest):
        if number == 1:
            approx = refine(lower)
        if number == 4:
            lifted = lift(lower, approx)
        if number == 6:
            write_leaf(lifted[0])
        if number == 8:
            write_nodes(range(LEVELS - 1), lifted)
        grown = split_dot(now, now[rank:])
        now = jnp.concatenate([now[:rank] + grown[:rank], grown[rank:]], axis=0)
    state[LEVELS] = now
    write_nodes([LEVELS - 1], lift([LEVELS], refine([LEVELS])))
    for copy in copies.values():
        copy.wait_send()
    for copy in outputs:
        copy.wait()


def hand_on(*refs):
    sources, targets, held, sem = refs[:3], refs[3:6], refs[6:9], refs[9]
    into, out = [], []
    for at, (source, middle, target) in enumerate(zip(sources, held, targets)):
        share = source.shape[-2] // SHARES
        for part in range(SHARES):
            place = (slice(None),) * (len(source.shape) - 2) + (pl.ds(part * share, share),)
            into.append(pltpu.make_async_copy(source.at[place], middle.at[place], sem.at[0, at, part]))
            out.append(pltpu.make_async_copy(middle.at[place], target.at[place], sem.at[1, at, part]))
    for copy in into:
        copy.start()
    for first, second in zip(into, out):
        first.wait()
        second.start()
    for copy in out:
        copy.wait()


def local(
    contributions,
    sketch_matrix,
    destinations,
    parent_rows,
    front_sizes,
    leaf_skeleton,
    merge_skeleton,
):
    fronts, leaves = lax.axis_size("front"), lax.axis_size("grp")
    devices = fronts * leaves
    rows, order = contributions.shape
    depth, width = sketch_matrix.shape
    rank = leaf_skeleton.shape[-1]
    count = devices // 2
    capacity = 2 * rows // devices
    lines = -(-capacity * (width // 128) // 16) * 16
    hbm = pl.BlockSpec(memory_space=pl.ANY)
    semaphores = [
        (fronts // 2 + 1,), (5,), (LEVELS + 2,), (fronts // 2,), (fronts // 2,), (CUTS, count), (CUTS, count), (2,),
        (devices,), (devices,), (LEVELS, width // 128), (LEVELS, width // 128),
    ]
    results = pl.pallas_call(
        functools.partial(whole_kernel, fronts, leaves, capacity),
        out_shape=(
            jax.ShapeDtypeStruct((PR_DEV, rank), jnp.float32),
            jax.ShapeDtypeStruct((LEVELS, 2 * rank, rank), jnp.float32),
            jax.ShapeDtypeStruct((rank, width), jnp.float32),
        ),
        in_specs=[hbm] * 7,
        out_specs=(hbm, hbm, hbm),
        scratch_shapes=[
            pltpu.VMEM((devices, rows), jnp.int32),
            pltpu.VMEM((devices, rows), jnp.int32),
            pltpu.SMEM((1,), jnp.int32),
            pltpu.VMEM((1, rank), jnp.int32),
            pltpu.VMEM((merge_skeleton.shape[1], 1, rank), jnp.int32),
            pltpu.VMEM((PR_DEV, rank), jnp.float32),
            pltpu.VMEM((LEVELS, 2 * rank, rank), jnp.float32),
            pltpu.VMEM((2, rows, order // 2), jnp.bfloat16),
            pltpu.VMEM((count, depth, width), jnp.bfloat16),
            pltpu.VMEM((2 * rows, width), jnp.float32),
            pltpu.VMEM((rows, width), jnp.float32),
            pltpu.VMEM((devices, lines, 128), jnp.bfloat16),
            pltpu.VMEM((devices, lines, 128), jnp.bfloat16),
            pltpu.VMEM((LEVELS, 2 * rank, width), jnp.float32),
            pltpu.VMEM((LEVELS + 1, rank, width), jnp.float32),
            pltpu.VMEM((LEVELS + 1, rank, rank), jnp.float32),
            pltpu.VMEM((LEVELS + 1, 2 * rank, rank), jnp.float32),
        ]
        + [pltpu.SemaphoreType.DMA(shape) for shape in semaphores],
        compiler_params=pltpu.CompilerParams(
            collective_id=0, has_side_effects=True, vmem_limit_bytes=62 * 2**20
        ),
        cost_estimate=pl.CostEstimate(
            flops=2 * rows * order * width, bytes_accessed=2 * rows * order, transcendentals=0
        ),
    )(
        contributions,
        sketch_matrix,
        destinations.reshape(devices, rows),
        parent_rows.reshape(devices, rows),
        front_sizes,
        leaf_skeleton[0],
        merge_skeleton.reshape(merge_skeleton.shape[1], 1, rank),
    )
    leaf_map, node_maps, top_rows = pl.pallas_call(
        hand_on,
        out_shape=[jax.ShapeDtypeStruct(result.shape, result.dtype) for result in results],
        in_specs=[hbm] * 3,
        out_specs=[hbm] * 3,
        scratch_shapes=[pltpu.VMEM(result.shape, result.dtype) for result in results]
        + [pltpu.SemaphoreType.DMA((2, 3, SHARES))],
        compiler_params=pltpu.CompilerParams(vmem_limit_bytes=62 * 2**20),
    )(*results)
    return (leaf_map[None], node_maps[None, None], top_rows[None, None])


def solution(mesh):
    in_specs = (
        P(("front", "grp"), None),
        P(("front", "grp"), None),
        P(),
        P(),
        P("front"),
        P("front", "grp", None),
        P("front", None, None),
    )
    out_specs = (
        P("front", "grp", None),
        P("front", "grp", None, None, None),
        P("front", "grp", None, None),
    )
    return jax.shard_map(local, mesh=mesh, in_specs=in_specs, out_specs=out_specs, check_vma=False)
```

```python
import functools
import heapq

import jax
import jax.numpy as jnp
from jax import lax
from jax.experimental import pallas as pl
from jax.experimental.pallas import tpu as pltpu
from jax.sharding import PartitionSpec as P

PR_DEV = 1024
LEVELS = 3
STEPS = 24
EXACT_STEPS = 1
CUTS = 4
SHARES = 4
HIGHEST = lax.Precision.HIGHEST
MESH = pl.DeviceIdType.MESH


def bits_of(count):
    return count.bit_length() - 1


def flip(value, mask):
    bit = 1
    while bit <= mask:
        if mask & bit:
            value = value + bit * (1 - 2 * lax.rem(lax.div(value, bit), 2))
        bit *= 2
    return value


def exchange_plan(grp_bits, x_bits, cuts):
    grp = [1 << b for b in reversed(range(grp_bits))]
    xs = [1 << (grp_bits + b) for b in reversed(range(x_bits))]
    half = grp_bits // 2
    near = grp[-half:]
    orders = (grp[:1] + xs + grp[1:], grp[:1] + near + grp[1 : len(grp) - half] + xs)
    link = {d: "x" if d in xs else "near" if d in near else "far" for d in grp + xs}
    free = {}
    events = []
    sequence = [(part, 0, orders[part % 2]) for part in range(cuts)]

    def send(now, part, slot, dim):
        begin = max(now, free.get(link[dim], 0.0))
        free[link[dim]] = begin + 1.0
        heapq.heappush(events, (begin + 1.0 + 0.2 * cuts, part, slot ^ dim))

    for place in range(grp_bits + x_bits):
        for part in range(cuts):
            send(0.0, part, 0, orders[part % 2][place])
    while events:
        now, part, slot = heapq.heappop(events)
        order = orders[part % 2]
        last = max([order.index(d) for d in order if d & slot], default=-1)
        onward = order[last + 1 :]
        sequence.append((part, slot, onward))
        for dim in onward:
            send(now, part, slot, dim)
    return sequence


def split(value):
    high = value.astype(jnp.bfloat16)
    return high, (value - high.astype(jnp.float32)).astype(jnp.bfloat16)


def halves(value):
    width = value.shape[1] // 2
    return value[:, :width] + value[:, width:]


def split_dot(left, right):
    lh, ll = split(left)
    rh, rl = split(right)
    both = jnp.concatenate([lh, ll], axis=1)
    top = jnp.concatenate([rh, rl], axis=1)
    low = jnp.concatenate([rh, jnp.zeros_like(rl)], axis=1)
    weights = jnp.concatenate([top, low], axis=0)
    return halves(jnp.dot(both, weights, preferred_element_type=jnp.float32))


def full_dot(left, right):
    return jnp.dot(left, right, precision=HIGHEST, preferred_element_type=jnp.float32)


def take_rows(picker, rows):
    width = rows.shape[1]
    high, rest = split(rows)
    rest = rows - high.astype(jnp.float32)
    middle, low = split(rest)
    parts = jnp.concatenate([high, middle, low], axis=1)
    found = jnp.dot(picker, parts, preferred_element_type=jnp.float32)
    return (found[:, :width] + found[:, width : 2 * width]) + found[:, 2 * width :]


def as_bf16(condition):
    return condition.astype(jnp.float32).astype(jnp.bfloat16)


def column_of(line):
    return jnp.transpose(jnp.broadcast_to(line.astype(jnp.float32), (128, line.shape[1])))


def whole_kernel(
    fronts, leaves, capacity,
    c_ref, omega_ref, dest_hbm, prow_hbm, size_hbm, leafskel_hbm, mergeskel_hbm,
    leaf_hbm, node_hbm, top_hbm,
    dest_ref, prow_ref, size_ref, leafskel_ref, mergeskel_ref, leaf_ref, node_ref,
    cols, slots, acc, partial, packed, arrived, stacks, bases, grams, state,
    local_sem, table_sem, out_sem, csend, crecv, send, recv, psem, asend, arecv, lsend, lrecv,
):
    front_at = lax.axis_index("front")
    grp_at = lax.axis_index("grp")
    core = lax.rem(front_at, 2)
    x_at = lax.div(front_at, 2)
    devices = fronts * leaves
    myself = front_at * leaves + grp_at
    x_count = fronts // 2
    grp_bits, x_bits = bits_of(leaves), bits_of(x_count)
    depth = omega_ref.shape[0]
    cut = depth // CUTS
    rows, width = c_ref.shape[0], omega_ref.shape[1]
    span = leaves * depth
    rank = leafskel_ref.shape[1]
    sibling = (x_at * 2 + 1 - core, grp_at)

    def device(number):
        return (lax.div(number, leaves), lax.rem(number, leaves))

    def partner(dim):
        if dim < leaves:
            return (front_at, flip(grp_at, dim))
        return (flip(x_at, dim // leaves) * 2 + core, grp_at)

    tables = [
        (dest_hbm, dest_ref), (prow_hbm, prow_ref), (size_hbm, size_ref),
        (leafskel_hbm, leafskel_ref), (mergeskel_hbm, mergeskel_ref),
    ]
    tables = [pltpu.make_async_copy(a, b, table_sem.at[at]) for at, (a, b) in enumerate(tables)]
    barrier = pltpu.get_barrier_semaphore()

    def greet(step, carry):
        other = device(lax.rem(myself + step, devices))
        pl.semaphore_signal(barrier, inc=1, device_id=other, device_id_type=MESH)
        return carry

    lax.fori_loop(1, devices, greet, 0)
    mine = []
    for x in range(x_count):
        begin = pl.multiple_of((x * 2 + core) * span, 128)
        copy = pltpu.make_async_copy(
            c_ref.at[:, pl.ds(begin, span)], cols.at[0, :, pl.ds(x * span, span)], local_sem.at[x]
        )
        copy.start()
        mine.append(copy)
    copy = pltpu.make_async_copy(omega_ref, slots.at[0], local_sem.at[x_count])
    copy.start()
    mine.append(copy)
    for copy in tables:
        copy.start()
    pl.semaphore_wait(barrier, devices - 1)

    def start(part, slot, dim):
        source = omega_ref if slot == 0 else slots.at[slot]
        copy = pltpu.make_async_remote_copy(
            src_ref=source.at[pl.ds(part * cut, cut), :],
            dst_ref=slots.at[slot ^ dim, pl.ds(part * cut, cut), :],
            send_sem=send.at[part, slot ^ dim],
            recv_sem=recv.at[part, slot ^ dim],
            device_id=partner(dim),
            device_id_type=MESH,
        )
        copy.start()
        return copy

    sequence = exchange_plan(grp_bits, x_bits, CUTS)
    arrivals = {}
    given = []
    for place in range(grp_bits + x_bits):
        for part, slot, onward in sequence[:CUTS]:
            arrivals[part, onward[place]] = start(part, slot, onward[place])
    for x in range(x_count):
        begin = pl.multiple_of((x * 2 + 1 - core) * span, 128)
        copy = pltpu.make_async_remote_copy(
            src_ref=c_ref.at[:, pl.ds(begin, span)],
            dst_ref=cols.at[1, :, pl.ds(x * span, span)],
            send_sem=csend.at[x],
            recv_sem=crecv.at[x],
            device_id=sibling,
            device_id_type=MESH,
        )
        copy.start()
        given.append(copy)

    acc[...] = jnp.zeros_like(acc)

    chunks = width // 128
    used = capacity * chunks
    lines = packed.shape[1]
    kept = capacity if capacity % 8 == 0 else lines

    shape = (devices, lines, rows)
    block_at = lax.broadcasted_iota(jnp.int32, shape, 0).astype(jnp.float32)
    line_at = lax.broadcasted_iota(jnp.int32, shape, 1)
    slot_at = jnp.where(line_at < used, lax.rem(line_at, capacity), -1).astype(jnp.float32)
    row = lax.broadcasted_iota(jnp.int32, (rows, rows), 0)
    col = lax.broadcasted_iota(jnp.int32, (rows, rows), 1)

    def make_tables():
        for copy in tables:
            copy.wait()
        going = dest_ref[pl.ds(myself, 1), :].astype(jnp.float32)
        same = (column_of(going)[:, :rows] == going) & (row < col)
        rank_in = jnp.sum(same.astype(jnp.float32), axis=0, keepdims=True)
        placing = as_bf16((block_at == going.reshape(1, 1, rows)) & (slot_at == rank_in.reshape(1, 1, rows)))
        placing = placing.reshape(devices * lines, rows)

        return placing

    def make_landing():
        coming = dest_ref[...] == myself
        ahead = jnp.dot(as_bf16(coming), as_bf16(row < col), preferred_element_type=jnp.float32)
        ahead = jnp.where(coming, ahead, -2.0)
        live = prow_ref[...] + grp_at * PR_DEV < size_ref[0]
        landing = jnp.where(live, prow_ref[...] + 1, 0).astype(jnp.float32)
        hit = ahead.reshape(devices, 1, rows) == slot_at[:, :kept, :]
        where_to = jnp.sum(jnp.where(hit, landing.reshape(devices, 1, rows), 0.0), axis=2, keepdims=True) - 1.0
        where_to = where_to.reshape(devices * kept, 1)
        where_to = jnp.transpose(jnp.broadcast_to(where_to, (devices * kept, 128)))[0:1, :]
        return where_to

    def make_picks(where_to):
        chosen = as_bf16(column_of(leafskel_ref[...])[:, 0:1] == where_to)
        picks = []
        for level in range(LEVELS):
            node = leaves - leaves // 2**level + lax.div(grp_at, 2 ** (level + 1))
            wanted = column_of(mergeskel_ref[node])[:, 0:1]
            at = lax.broadcasted_iota(jnp.int32, (rank, 2 * rank), 1).astype(jnp.float32)
            picks.append(as_bf16(wanted == at))
        return chosen, picks

    def multiply(slot):
        x_from = flip(x_at, slot // leaves)
        grp_from = flip(grp_at, slot % leaves)
        begin = pl.multiple_of((x_from * leaves + grp_from) * depth, 128)
        left = cols[:, :, pl.ds(begin, depth)].reshape(2 * rows, depth)
        acc[...] += jnp.dot(left, slots[slot], preferred_element_type=jnp.float32)

    held = {}
    ready = False
    waiting = []
    for number, (part, slot, onward) in enumerate(sequence):
        if slot != 0:
            arrivals[part, slot].wait_recv()
            for dim in onward:
                arrivals[part, slot ^ dim] = start(part, slot, dim)
        held[slot] = held.get(slot, 0) + 1
        if held[slot] == CUTS:
            waiting.append(slot)
        if number >= len(sequence) // 4:
            if not ready:
                for copy in mine:
                    copy.wait()
                for copy in given:
                    copy.wait_recv()
                ready = True
            if waiting:
                multiply(waiting.pop(0))
        if number == len(sequence) // 2:
            placing = make_tables()
        if number == len(sequence) * 5 // 8:
            where_to = make_landing()
        if number == len(sequence) * 3 // 4:
            chosen, picks = make_picks(where_to)
    for item in waiting:
        multiply(item)

    final = pltpu.make_async_remote_copy(
        src_ref=acc.at[pl.ds(rows, rows), :],
        dst_ref=partial,
        send_sem=psem.at[0],
        recv_sem=psem.at[1],
        device_id=sibling,
        device_id_type=MESH,
    )
    final.start()
    final.wait_recv()
    sketch = (acc[pl.ds(0, rows), :] + partial[...]).astype(jnp.bfloat16)

    placed = jnp.dot(placing, sketch, preferred_element_type=jnp.float32).reshape(devices, lines, width)
    line = lax.broadcasted_iota(jnp.int32, (devices, lines, 128), 1)
    chunk_at = lax.div(line, capacity)
    sent = placed[:, :, :128]
    for chunk in range(1, chunks):
        sent = jnp.where(chunk_at == chunk, placed[:, :, chunk * 128 : (chunk + 1) * 128], sent)
    packed[...] = sent.astype(jnp.bfloat16)

    def deliver(step):
        number = lax.rem(myself + step, devices)
        return pltpu.make_async_remote_copy(
            src_ref=packed.at[number],
            dst_ref=arrived.at[myself],
            send_sem=asend.at[step],
            recv_sem=arecv.at[step],
            device_id=device(number),
            device_id_type=MESH,
        )

    for step in range(1, devices):
        deliver(step).start()
    arrived[pl.ds(myself, 1)] = packed[pl.ds(myself, 1)]

    def deliver_end(step, carry):
        deliver(step).wait_send()
        return carry

    def deliver_wait(step, carry):
        number = lax.rem(myself + devices - step, devices)
        pltpu.make_async_remote_copy(
            src_ref=packed.at[number],
            dst_ref=arrived.at[number],
            send_sem=asend.at[step],
            recv_sem=arecv.at[step],
            device_id=device(number),
            device_id_type=MESH,
        ).wait_recv()
        return carry

    for copy in given + list(arrivals.values()) + [final]:
        copy.wait_send()
    lax.fori_loop(1, devices, deliver_wait, 0)
    flat = arrived[...].astype(jnp.float32)
    if kept == capacity:
        wide = [flat[:, chunk * capacity : (chunk + 1) * capacity] for chunk in range(chunks)]
    else:
        wide = [jnp.where(chunk_at == chunk, flat, 0.0) for chunk in range(chunks)]
    landed = jnp.concatenate(wide, axis=2).reshape(devices * kept, width).astype(jnp.bfloat16)

    eye_row = lax.broadcasted_iota(jnp.int32, (rank, rank), 0)
    ident = (eye_row == lax.broadcasted_iota(jnp.int32, (rank, rank), 1)).astype(jnp.float32)

    def offer(level, chunk, basis):
        side = lax.rem(lax.div(grp_at, 2**level), 2)
        place = pl.ds(pl.multiple_of(side * rank, rank), rank)
        columns = pl.ds(chunk * 128, 128)
        bases[level, :, columns] = basis
        stacks[level, place, columns] = basis
        copy = pltpu.make_async_remote_copy(
            src_ref=stacks.at[level, place, columns],
            dst_ref=stacks.at[level, place, columns],
            send_sem=lsend.at[level, chunk],
            recv_sem=lrecv.at[level, chunk],
            device_id=(front_at, flip(grp_at, 2**level)),
            device_id_type=MESH,
        )
        copy.start()
        copies[level, chunk] = copy

    def merge(level, chunk):
        copies[level, chunk].wait_recv()
        columns = pl.ds(chunk * 128, 128)
        basis = take_rows(picks[level], stacks[level, :, columns])
        if level < LEVELS - 1:
            offer(level + 1, chunk, basis)
        else:
            bases[LEVELS, :, columns] = basis

    def begin_solve(at):
        basis = bases[at]
        gram = lax.dot_general(
            basis, basis, (((1,), (1,)), ((), ())), precision=HIGHEST, preferred_element_type=jnp.float32
        )
        trace = jnp.sum(gram * ident, keepdims=True)
        shift = 0.1 * (trace / rank) + 1e-05
        gram = gram + shift * ident
        scale = 1.0 / (trace + rank * shift)
        grams[at] = gram
        rest = ident - gram * scale
        state[at, pl.ds(0, rank), :] = (ident + rest) * scale
        state[at, pl.ds(rank, rank), :] = split_dot(rest, rest)

    def advance(systems, count):
        def step(_, carry):
            for at in systems:
                now = state[at]
                grown = split_dot(now, now[rank:])
                state[at, pl.ds(0, rank), :] = now[:rank] + grown[:rank]
                state[at, pl.ds(rank, rank), :] = grown[rank:]
            return carry

        lax.fori_loop(0, count, step, 0)

    def refine(systems):
        approx = {at: state[at, pl.ds(0, rank), :] for at in systems}
        for _ in range(EXACT_STEPS):
            inner = {at: 2.0 * ident - full_dot(grams[at], approx[at]) for at in systems}
            approx = {at: full_dot(approx[at], inner[at]) for at in systems}
        return approx

    def lift(systems, approx):
        return {at: full_dot(jnp.transpose(bases[at]), approx[at]) for at in systems}

    def put(source, target, at):
        copy = pltpu.make_async_copy(source, target, out_sem.at[at])
        copy.start()
        return copy

    def write_leaf(lifted):
        small = halves(jnp.dot(landed, jnp.concatenate(split(lifted), axis=1), preferred_element_type=jnp.float32))
        small = jnp.concatenate(split(small), axis=1)
        spot = lax.broadcasted_iota(jnp.int32, (leaf_ref.shape[0], devices * kept), 0).astype(jnp.float32)
        leaf_ref[...] = halves(jnp.dot(as_bf16(spot == where_to), small, preferred_element_type=jnp.float32))
        outputs.append(put(leaf_ref, leaf_hbm, LEVELS))

    def write_nodes(levels, lifted):
        for level in levels:
            node_ref[level] = split_dot(stacks[level], lifted[level + 1])
        for level in levels:
            outputs.append(put(node_ref.at[level], node_hbm.at[level], level))

    outputs = []
    copies = {}
    total = STEPS - EXACT_STEPS - 1
    first, second, third = total // 4, total // 7, total // 10
    leaf_basis = jnp.dot(chosen, landed, preferred_element_type=jnp.float32)
    for chunk in range(chunks):
        offer(0, chunk, leaf_basis[:, chunk * 128 : (chunk + 1) * 128])
    begin_solve(0)
    advance([0], first)
    for chunk in range(chunks):
        merge(0, chunk)
        if chunk == 0:
            advance([0], second)
    begin_solve(1)
    for chunk in range(chunks):
        merge(1, chunk)
        if chunk == 0:
            advance([0, 1], third)
    begin_solve(2)
    left = total - first - second - third
    advance([0, 1, 2], left)
    lax.fori_loop(1, devices, deliver_end, 0)
    for chunk in range(chunks):
        merge(2, chunk)
    outputs.append(put(bases.at[LEVELS], top_hbm, LEVELS + 1))
    begin_solve(3)
    more = total - third - left
    advance([1, 2, 3], more)
    rest = total - left - more
    advance([2, 3], rest)
    now = state[LEVELS]
    lower = list(range(LEVELS))
    for number in range(total - more - rest):
        if number == 1:
            approx = refine(lower)
        if number == 4:
            lifted = lift(lower, approx)
        if number == 6:
            write_leaf(lifted[0])
        if number == 8:
            write_nodes(range(LEVELS - 1), lifted)
        grown = split_dot(now, now[rank:])
        now = jnp.concatenate([now[:rank] + grown[:rank], grown[rank:]], axis=0)
    state[LEVELS] = now
    write_nodes([LEVELS - 1], lift([LEVELS], refine([LEVELS])))
    for copy in copies.values():
        copy.wait_send()
    for copy in outputs:
        copy.wait()


def hand_on(*refs):
    sources, targets, held, sem = refs[:3], refs[3:6], refs[6:9], refs[9]
    into, out = [], []
    for at, (source, middle, target) in enumerate(zip(sources, held, targets)):
        share = source.shape[-2] // SHARES
        for part in range(SHARES):
            place = (slice(None),) * (len(source.shape) - 2) + (pl.ds(part * share, share),)
            into.append(pltpu.make_async_copy(source.at[place], middle.at[place], sem.at[0, at, part]))
            out.append(pltpu.make_async_copy(middle.at[place], target.at[place], sem.at[1, at, part]))
    for copy in into:
        copy.start()
    for first, second in zip(into, out):
        first.wait()
        second.start()
    for copy in out:
        copy.wait()


def local(
    contributions,
    sketch_matrix,
    destinations,
    parent_rows,
    front_sizes,
    leaf_skeleton,
    merge_skeleton,
):
    fronts, leaves = lax.axis_size("front"), lax.axis_size("grp")
    devices = fronts * leaves
    rows, order = contributions.shape
    depth, width = sketch_matrix.shape
    rank = leaf_skeleton.shape[-1]
    count = devices // 2
    capacity = 2 * rows // devices
    lines = -(-capacity * (width // 128) // 16) * 16
    hbm = pl.BlockSpec(memory_space=pl.ANY)
    semaphores = [
        (fronts // 2 + 1,), (5,), (LEVELS + 2,), (fronts // 2,), (fronts // 2,), (CUTS, count), (CUTS, count), (2,),
        (devices,), (devices,), (LEVELS, width // 128), (LEVELS, width // 128),
    ]
    results = pl.pallas_call(
        functools.partial(whole_kernel, fronts, leaves, capacity),
        out_shape=(
            jax.ShapeDtypeStruct((PR_DEV, rank), jnp.float32),
            jax.ShapeDtypeStruct((LEVELS, 2 * rank, rank), jnp.float32),
            jax.ShapeDtypeStruct((rank, width), jnp.float32),
        ),
        in_specs=[hbm] * 7,
        out_specs=(hbm, hbm, hbm),
        scratch_shapes=[
            pltpu.VMEM((devices, rows), jnp.int32),
            pltpu.VMEM((devices, rows), jnp.int32),
            pltpu.SMEM((1,), jnp.int32),
            pltpu.VMEM((1, rank), jnp.int32),
            pltpu.VMEM((merge_skeleton.shape[1], 1, rank), jnp.int32),
            pltpu.VMEM((PR_DEV, rank), jnp.float32),
            pltpu.VMEM((LEVELS, 2 * rank, rank), jnp.float32),
            pltpu.VMEM((2, rows, order // 2), jnp.bfloat16),
            pltpu.VMEM((count, depth, width), jnp.bfloat16),
            pltpu.VMEM((2 * rows, width), jnp.float32),
            pltpu.VMEM((rows, width), jnp.float32),
            pltpu.VMEM((devices, lines, 128), jnp.bfloat16),
            pltpu.VMEM((devices, lines, 128), jnp.bfloat16),
            pltpu.VMEM((LEVELS, 2 * rank, width), jnp.float32),
            pltpu.VMEM((LEVELS + 1, rank, width), jnp.float32),
            pltpu.VMEM((LEVELS + 1, rank, rank), jnp.float32),
            pltpu.VMEM((LEVELS + 1, 2 * rank, rank), jnp.float32),
        ]
        + [pltpu.SemaphoreType.DMA(shape) for shape in semaphores],
        compiler_params=pltpu.CompilerParams(
            collective_id=0, has_side_effects=True, vmem_limit_bytes=62 * 2**20
        ),
        cost_estimate=pl.CostEstimate(
            flops=2 * rows * order * width, bytes_accessed=2 * rows * order, transcendentals=0
        ),
    )(
        contributions,
        sketch_matrix,
        destinations.reshape(devices, rows),
        parent_rows.reshape(devices, rows),
        front_sizes,
        leaf_skeleton[0],
        merge_skeleton.reshape(merge_skeleton.shape[1], 1, rank),
    )
    leaf_map, node_maps, top_rows = pl.pallas_call(
        hand_on,
        out_shape=[jax.ShapeDtypeStruct(result.shape, result.dtype) for result in results],
        in_specs=[hbm] * 3,
        out_specs=[hbm] * 3,
        scratch_shapes=[pltpu.VMEM(result.shape, result.dtype) for result in results]
        + [pltpu.SemaphoreType.DMA((2, 3, SHARES))],
        compiler_params=pltpu.CompilerParams(vmem_limit_bytes=62 * 2**20),
    )(*results)
    return (leaf_map[None], node_maps[None, None], top_rows[None, None])


def solution(mesh):
    in_specs = (
        P(("front", "grp"), None),
        P(("front", "grp"), None),
        P(),
        P(),
        P("front"),
        P("front", "grp", None),
        P("front", None, None),
    )
    out_specs = (
        P("front", "grp", None),
        P("front", "grp", None, None, None),
        P("front", "grp", None, None),
    )
    return jax.shard_map(local, mesh=mesh, in_specs=in_specs, out_specs=out_specs, check_vma=False)
```
